256 devices in a mesh: seq: 64 (over z, y_lo, x), tp: 4 (over y_hi, core).
Axes of the slice: x: 4, y: 4 (y_hi: 2, y_lo: 2; y = y_hi * 2 + y_lo), z: 8, core: 2. Of those that a mesh axis runs over, the one named last changes fastest.
Arguments:
- latent: bfloat16 [64, 128, 4096], P('seq', None, 'tp'), may hold values from -6 to 6
- direction: bfloat16 [64, 128, 4096], P('seq', None, 'tp'), may hold values from -6 to 6
- concept: int32 [64], P('seq'), may hold values from 0 to 255
- timestep: int32 [64], replicated, may hold values from 0 to 999
- concept_table: bfloat16 [256, 4096], P(None, 'tp'), may hold values from -1.5 to 1.5
- w_query: bfloat16 [4096, 2048], P(None, 'tp'), may hold values from -2 to 2
- w_key: bfloat16 [4096, 2048], P(None, 'tp'), may hold values from -2 to 2
Outputs:
- score_field: bfloat16 [64, 128, 4096], P('seq', None, 'tp')
- table_grad: float32 [256, 4096], P(None, ('seq', 'tp'))
The draws below stay inside these ranges and needn't reach their ends.
All inputs are finite; a program needn't handle non-finite values.
Results may differ from the reference program's by a relative error of at most 0.015.
Values may be sent and summed in bfloat16 or wider, within the bound.
No kernel may reach another device: no remote copies, remote signals or barrier semaphores. Data moves between devices by JAX's collectives and lax.ppermute only.
A program may use at most 64 MiB of HBM per device.

```python
import math
import jax
import jax.numpy as jnp
from jax import lax

D = 4096
HEADS = 16
HD = 128
CONCEPTS = 256
STEPS = 1000
POS = 128
FRAMES = 64


def shared_base(key):
    base = jax.random.normal(key, (D, HEADS * HD), jnp.float32)
    return jnp.clip(base, -6.0, 6.0) / jnp.sqrt(jnp.float32(D))


def draw_w_query(key, part):
    base = shared_base(key)
    return base.astype(jnp.bfloat16)


def draw_w_key(key, part):
    key = jax.random.fold_in(key, 7)
    own = jnp.clip(jax.random.normal(key, (D, HEADS * HD), jnp.float32), -6.0, 6.0) / jnp.sqrt(jnp.float32(D))
    weight = own
    return weight.astype(jnp.bfloat16)


def plant(result, stream_key, low, high):
    extent = result.shape
    spot = [jax.random.randint(jax.random.fold_in(stream_key, axis), (), 0, extent[axis]) for axis in range(len(extent))]
    result = result.at[tuple(spot)].set(low)
    longest = extent.index(max(extent))
    spot[longest] = (spot[longest] + 1) % extent[longest]
    return result.at[tuple(spot)].set(high)


def shard_levels(key, shape, shards, smallest, largest):
    factor_of, own = 1.0, jax.random.fold_in(key, 6)
    for position, shards_of in shards:
        heights = jnp.exp(jax.random.uniform(jax.random.fold_in(own, position), (shards_of,), jnp.float32, smallest / len(shards), largest / len(shards)))
        factor_of = factor_of * jnp.repeat(heights, shape[position] // shards_of).reshape([-1 if axis == position else 1 for axis in range(len(shape))])
    return factor_of


def noise(own_key, shape, width, reach, split=(), kind=jnp.bfloat16):
    values = jax.random.normal(own_key, shape, jnp.float32) * width
    if len(split) > 0:
        values = shard_levels(own_key, shape, split, -0.22, 0.18) * values
    return jnp.clip(values, min=-reach, max=reach).astype(kind)


def setup_inputs(seed: int = 0) -> dict:
    splits = jax.random.split(jax.random.key(seed), 8)
    return {
        "latent": noise(splits[0], (FRAMES, POS, D), 1.0, 6.0, ((0, 64), (2, 4))),
        "direction": noise(splits[1], (FRAMES, POS, D), 1.0, 6.0, ((0, 64), (2, 4))),
        "concept": plant(jax.random.randint(splits[2], (FRAMES,), 0, CONCEPTS), jax.random.fold_in(splits[2], 1), 0, CONCEPTS - 1).astype(jnp.int32),
        "timestep": plant(jax.random.randint(splits[3], (FRAMES,), 0, STEPS), jax.random.fold_in(splits[3], 1), 0, STEPS - 1).astype(jnp.int32),
        "concept_table": noise(splits[4], (CONCEPTS, D), 0.3, 1.5, ((1, 4),)),
        "w_query": draw_w_query(jax.random.fold_in(splits[7], 71), 0),
        "w_key": draw_w_key(jax.random.fold_in(splits[7], 71), 0),
    }


EPS = 1e-06

def normalize(values, tangent):
    mean_sq = lax.optimization_barrier(jnp.mean(values * values, axis=-1, keepdims=True))
    inv_rms = lax.rsqrt(mean_sq + EPS)
    normed = values * inv_rms
    normed_tan = inv_rms * (tangent - normed * lax.optimization_barrier(jnp.mean(normed * tangent, axis=-1, keepdims=True)))
    return (normed, normed_tan, inv_rms)

def energy_cotangents(query_rows, key_rows, query_tan, key_tan, inv_temp):
    query_f = query_rows.astype(jnp.float32)
    key_f = key_rows.astype(jnp.float32)
    qtan_f = query_tan.astype(jnp.float32)
    ktan_f = key_tan.astype(jnp.float32)
    temp_b = inv_temp[None, None, :, None]
    scores = jnp.einsum('fphd,gphd->phfg', query_f, key_f) * temp_b
    top = lax.optimization_barrier(jnp.max(scores, axis=-1, keepdims=True))
    weights = jnp.exp(scores - top)
    weights = weights / lax.optimization_barrier(jnp.sum(weights, axis=-1, keepdims=True))
    tangent_dot = jnp.einsum('fphd,gphd->phfg', qtan_f, key_f) + jnp.einsum('fphd,gphd->phfg', query_f, ktan_f)
    mean_tan = lax.optimization_barrier(jnp.sum(weights * tangent_dot, axis=-1, keepdims=True))
    curvature = -temp_b * weights * (tangent_dot - mean_tan)
    grad_query = -jnp.einsum('phfg,gphd->fphd', weights, key_f)
    grad_key = -jnp.einsum('phfg,fphd->gphd', weights, query_f)
    adj_query = jnp.einsum('phfg,gphd->fphd', curvature, key_f) - jnp.einsum('phfg,gphd->fphd', weights, ktan_f)
    adj_key = jnp.einsum('phfg,fphd->gphd', curvature, query_f) - jnp.einsum('phfg,fphd->gphd', weights, qtan_f)
    return (adj_query.astype(jnp.bfloat16), adj_key.astype(jnp.bfloat16), grad_query.astype(jnp.bfloat16), grad_key.astype(jnp.bfloat16))

def project(inputs, weight):
    flat = inputs.reshape(-1, inputs.shape[-1])
    out = jnp.dot(flat, weight, preferred_element_type=jnp.float32).astype(jnp.bfloat16)
    return out.reshape(inputs.shape[0], inputs.shape[1], -1, HD)

def project_back(first, first_w, second, second_w):
    lead = first.shape[0] * first.shape[1]
    part_one = jnp.dot(first.reshape(lead, -1), first_w.T, preferred_element_type=jnp.float32)
    part_two = jnp.dot(second.reshape(lead, -1), second_w.T, preferred_element_type=jnp.float32)
    return (part_one + part_two).reshape(first.shape[0], first.shape[1], -1)

def reference(latent, direction, concept, timestep, concept_table, w_query, w_key):
    values = latent.astype(jnp.float32)
    tangent = direction.astype(jnp.float32)
    normed, normed_tan, inv_rms = normalize(values, tangent)
    onehot = (concept[:, None] == jnp.arange(CONCEPTS, dtype=jnp.int32)[None, :]).astype(jnp.float32)
    modul = 1.0 + jnp.dot(onehot, concept_table.astype(jnp.float32), precision=lax.Precision.HIGHEST)
    hidden = (normed * modul[:, None, :]).astype(jnp.bfloat16)
    hidden_tan = (normed_tan * modul[:, None, :]).astype(jnp.bfloat16)
    query_rows = project(hidden, w_query)
    key_rows = project(hidden, w_key)
    query_tan = project(hidden_tan, w_query)
    key_tan = project(hidden_tan, w_key)
    inv_temp = (0.25 + 1.75 * timestep.astype(jnp.float32) / STEPS) / math.sqrt(HD)
    adj_query, adj_key, grad_query, grad_key = energy_cotangents(query_rows, key_rows, query_tan, key_tan, inv_temp)
    units = project_back(grad_query, w_query, grad_key, w_key)
    drift = project_back(adj_query, w_query, adj_key, w_key)
    gain = modul[:, None, :] * units
    score_field = (inv_rms * (gain - normed * lax.optimization_barrier(jnp.mean(gain * normed, axis=-1, keepdims=True)))).astype(jnp.bfloat16)
    terms = lax.optimization_barrier(jnp.sum(normed * drift + normed_tan * units, axis=1))
    table_grad = jnp.dot(onehot.T, terms, precision=lax.Precision.HIGHEST)
    return (score_field, table_grad)
```

```python
import functools
import math

import jax
import jax.numpy as jnp
from jax import lax
from jax.experimental import pallas as pl
from jax.experimental.pallas import tpu as pltpu
from jax.sharding import PartitionSpec as P

D = 4096
HD = 128
CONCEPTS = 256
STEPS = 1000
EPS = 1e-06
F = 64
W = 1024
ROWS = 208

BF = jnp.bfloat16
F32 = jnp.float32
NT = (((1,), (1,)), ((), ()))
TN = (((0,), (0,)), ((), ()))


def nt(a, b):
    return lax.dot_general(a, b, NT, preferred_element_type=F32)


def main_kernel(me_ref, c0, c1, c2, c3, t0, t1, t2, t3, concept_ref, temp_ref, wq_ref, wk_ref,
                rs_ref, stat_ref, w_s, mod_s, h_s, acc_s, g_s, sems):
    parts = (c0, c1, c2, c3)
    tables = (t0, t1, t2, t3)
    me = me_ref[0]
    copies = []
    for k in range(4):
        rows = pl.ds(pl.multiple_of((me ^ k) * W, W), W)
        a = pltpu.make_async_copy(wq_ref.at[rows], w_s.at[k, :, pl.ds(0, 512)], sems.at[2 * k])
        b = pltpu.make_async_copy(wk_ref.at[rows], w_s.at[k, :, pl.ds(512, 512)], sems.at[2 * k + 1])
        a.start()
        b.start()
        copies.append((a, b))
    onehot = (concept_ref[...] == lax.broadcasted_iota(jnp.int32, (F, CONCEPTS), 1)).astype(BF)
    sq = jnp.zeros((2, F, 128), F32)
    sd = jnp.zeros((2, F, 128), F32)
    for k in range(4):
        mod_s[k] = 1.0 + jnp.dot(onehot, tables[k][...], preferred_element_type=F32)
        for j in range(8):
            lanes = pl.ds(128 * j, 128)
            x = parts[k][0:2, :, lanes].astype(F32)
            d = parts[k][2:4, :, lanes].astype(F32)
            sq = sq + x * x
            sd = sd + x * d
    inv = lax.rsqrt(jnp.sum(sq, axis=-1, keepdims=True) / D + EPS)
    mean = inv * (jnp.sum(sd, axis=-1, keepdims=True) / D)
    inv2 = inv.reshape(2 * F, 1)
    mean2 = mean.reshape(2 * F, 1)

    def normed_of(k, lanes):
        x = parts[k][0:2, :, lanes].astype(F32).reshape(2 * F, -1)
        d = parts[k][2:4, :, lanes].astype(F32).reshape(2 * F, -1)
        n = x * inv2
        return n, inv2 * (d - n * mean2)

    for k in range(4):
        for j in range(4):
            lanes = pl.ds(256 * j, 256)
            n, nd = normed_of(k, lanes)
            m = mod_s[k, :, lanes]
            m = jnp.concatenate([m, m], axis=0)
            h_s[k, 0:128, lanes] = (n * m).astype(BF)
            h_s[k, 128:256, lanes] = (nd * m).astype(BF)
    for k in range(4):
        copies[k][0].wait()
        copies[k][1].wait()

    acc_s[...] = jnp.zeros_like(acc_s)

    def forward(k, carry):
        acc_s[...] += jnp.dot(h_s[k], w_s[k], preferred_element_type=F32)
        return carry

    lax.fori_loop(0, 4, forward, 0)

    temp = temp_ref[...]
    scal = jnp.zeros((2 * F, 128), F32)
    scals = []
    for p in range(2):
        part = jnp.zeros((F, HD), F32)
        for h in range(4):
            ql, kl = pl.ds(128 * h, 128), pl.ds(512 + 128 * h, 128)
            r0, r1 = pl.ds(64 * p, 64), pl.ds(128 + 64 * p, 64)
            q, qt = acc_s[r0, ql].astype(BF), acc_s[r1, ql].astype(BF)
            kk, kt = acc_s[r0, kl].astype(BF), acc_s[r1, kl].astype(BF)
            prod = nt(jnp.concatenate([q, qt], axis=0), jnp.concatenate([kk, kt], axis=0))
            scores = prod[0:64, 0:64] * temp
            tdot = prod[64:128, 0:64] + prod[0:64, 64:128]
            e = jnp.exp(scores - jnp.max(scores, axis=-1, keepdims=True))
            w = e / jnp.sum(e, axis=-1, keepdims=True)
            cur = -temp * w * (tdot - jnp.sum(w * tdot, axis=-1, keepdims=True))
            wc = jnp.concatenate([w, cur], axis=0).astype(BF)
            wct = jnp.concatenate([w, cur], axis=1).T.astype(BF)
            back_q = jnp.dot(wc, jnp.concatenate([kk, kt], axis=1), preferred_element_type=F32)
            back_k = jnp.dot(wct, jnp.concatenate([q, qt], axis=1), preferred_element_type=F32)
            gq, aq = -back_q[0:64, 0:128], back_q[64:128, 0:128] - back_q[0:64, 128:256]
            gk, ak = -back_k[0:64, 0:128], back_k[64:128, 0:128] - back_k[0:64, 128:256]
            gqb, gkb = gq.astype(BF), gk.astype(BF)
            g_s[r0, ql] = gqb
            g_s[r1, ql] = aq.astype(BF)
            g_s[r0, kl] = gkb
            g_s[r1, kl] = ak.astype(BF)
            part = part + gqb.astype(F32) * q.astype(F32) + gkb.astype(F32) * kk.astype(F32)
        scals.append(jnp.sum(part, axis=-1, keepdims=True))
    scal = jnp.concatenate(scals, axis=0)
    eye = lax.broadcasted_iota(jnp.int32, (128, 128), 0) == lax.broadcasted_iota(jnp.int32, (128, 128), 1)
    srow = jnp.sum(jnp.where(eye, scal, 0.0), axis=0, keepdims=True)
    hi = srow.astype(BF).astype(F32)
    lo = srow - hi
    sub = lax.broadcasted_iota(jnp.int32, (16, 128), 0)
    stats = jnp.where(sub == 0, hi, jnp.where(sub == 1, lo, 0.0))
    lane = lax.broadcasted_iota(jnp.int32, (2 * F, 128), 1)
    stat_ref[...] = jnp.where(lane == 0, inv2, 0.0)

    rr = lax.broadcasted_iota(jnp.int32, (256, 512), 0)
    cc = lax.broadcasted_iota(jnp.int32, (256, 512), 1)
    source = ((rr >> 3) & 7) * 64 + (rr >> 6) * 16 + (rr & 7)
    perm_a = (cc == source).astype(BF)
    perm_b = (cc == source + 8).astype(BF)
    for k in range(4):
        rs_ref[k, 192:208, :] = jnp.concatenate([stats] + [jnp.zeros((16, 896), F32)], axis=1).astype(BF)
    for k in range(4):
        for j in range(2):
            lanes = pl.ds(512 * j, 512)
            back = nt(g_s[...], w_s[k, 512 * j:512 * j + 512, :])
            units, drift = back[0:128], back[128:256]
            rs_ref[k, 0:128, lanes] = units.astype(BF)
            n, nd = normed_of(k, lanes)
            terms = n * drift + nd * units
            terms = (terms[0:64] + terms[64:128]).astype(BF)
            moved = jnp.concatenate([nt(perm_a, terms), nt(perm_b, terms)], axis=1).astype(BF)
            spot = pl.ds(pl.multiple_of(((me ^ k) * 2 + j) * 128, 128), 128)
            for t in range(4):
                rs_ref[me ^ t, 128:192, spot] = moved[64 * t:64 * t + 64]


def main_call(me, parts, tables, concept, temp, wq, wk):
    vm = pl.BlockSpec(memory_space=pltpu.VMEM)
    sm = pl.BlockSpec(memory_space=pltpu.SMEM)
    hb = pl.BlockSpec(memory_space=pl.ANY)
    return pl.pallas_call(
        main_kernel,
        out_shape=(jax.ShapeDtypeStruct((4, ROWS, W), BF), jax.ShapeDtypeStruct((2 * F, 128), F32)),
        in_specs=[sm] + [vm] * 10 + [hb, hb],
        out_specs=(vm, vm),
        scratch_shapes=[
            pltpu.VMEM((4, W, W), BF),
            pltpu.VMEM((4, F, W), F32),
            pltpu.VMEM((4, 256, W), BF),
            pltpu.VMEM((256, W), F32),
            pltpu.VMEM((256, W), BF),
            pltpu.SemaphoreType.DMA((8,)),
        ],
        compiler_params=pltpu.CompilerParams(vmem_limit_bytes=48 * 1024 * 1024),
        name="attend",
    )(me, *parts, *tables, concept, temp, wq, wk)


def merge_kernel(a_ref, b_ref, o_ref):
    o_ref[0:192, :] = (a_ref[0:192, :].astype(F32) + b_ref[0:192, :].astype(F32)).astype(BF)
    o_ref[192:208, :] = jnp.concatenate(
        [a_ref[192:208, 0:128], b_ref[192:208, 0:128], a_ref[192:208, 256:1024]], axis=1)


def final_kernel(a_ref, b_ref, c_ref, x_ref, table_ref, concept_ref, stat_ref, score_ref, terms_ref):
    total = (a_ref[0:192, :].astype(F32) + b_ref[0:192, :].astype(F32)) + c_ref[0:192, :].astype(F32)
    terms_ref[...] = total[128:192].astype(BF)
    units = total[0:128]
    srow = jnp.zeros((1, 128), F32)
    for ref, lane in ((a_ref, 0), (b_ref, 0), (c_ref, 0), (c_ref, 128)):
        part = ref[192:208, lane:lane + 128].astype(F32)
        srow = srow + (part[0:1] + part[1:2])
    eye = lax.broadcasted_iota(jnp.int32, (128, 128), 0) == lax.broadcasted_iota(jnp.int32, (128, 128), 1)
    mean = jnp.sum(jnp.where(eye, srow, 0.0), axis=1, keepdims=True) / D
    inv = jnp.sum(stat_ref[...], axis=1, keepdims=True)
    onehot = (concept_ref[...] == lax.broadcasted_iota(jnp.int32, (F, CONCEPTS), 1)).astype(BF)
    mod = 1.0 + jnp.dot(onehot, table_ref[...], preferred_element_type=F32)
    mod = jnp.concatenate([mod, mod], axis=0)
    x = x_ref[0:2].astype(F32).reshape(2 * F, W)
    score_ref[...] = (inv * (mod * units - (x * inv) * mean)).astype(BF).reshape(2, F, W)


def body(latent, direction, concept, timestep, concept_table, w_query, w_key):
    tp = lax.axis_index("tp")
    y_hi = tp >> 1
    cross = []
    for s in range(64):
        for t in range(4):
            cross.append((4 * s + t, 4 * (s ^ 4) + (t ^ 2)))
    core = [(t, t ^ 1) for t in range(4)]
    swap_core = lambda v: lax.ppermute(v, "tp", core)
    swap_chip = lambda v: lax.ppermute(v, ("seq", "tp"), cross)

    def flip(v):
        v = v.reshape((8, 2, 4) + v.shape[1:])
        v = jnp.where(y_hi == 1, v[:, ::-1], v)
        return v.reshape((64,) + v.shape[3:])

    mine = jnp.concatenate([latent.reshape(F, 2, W), direction.reshape(F, 2, W)], axis=1)
    ident = jnp.broadcast_to(concept.astype(BF).reshape(1, 1, 1), (F, 4, 128))
    sent = jnp.concatenate([flip(mine), ident], axis=2)
    got = lax.all_to_all(sent, "seq", split_axis=0, concat_axis=0, tiled=True)
    ids = got[:, 0, W:W + 1].astype(jnp.int32)
    own = jnp.transpose(got[:, :, :W], (1, 0, 2))

    t_own = concept_table
    t_core = swap_core(t_own)
    t_chip = swap_chip(t_own)
    t_both = swap_core(t_chip)

    chip = swap_chip(own)
    near = swap_core(own)
    both = swap_core(chip)

    temp = ((0.25 + 1.75 * timestep.astype(F32) / STEPS) / math.sqrt(HD)).reshape(F, 1)
    parts, stat = main_call(
        tp.reshape(1).astype(jnp.int32), (own, near, chip, both), (t_own, t_core, t_chip, t_both), ids, temp, w_query, w_key)

    vm = pl.BlockSpec(memory_space=pltpu.VMEM)
    far = swap_core(parts[3])
    summed = pl.pallas_call(
        merge_kernel, out_shape=jax.ShapeDtypeStruct((ROWS, W), BF), in_specs=[vm] * 2, out_specs=vm, name="merge",
    )(parts[2], far)
    arrived = swap_chip(summed)
    beside = swap_core(parts[1])
    score, terms = pl.pallas_call(
        final_kernel,
        out_shape=(jax.ShapeDtypeStruct((2, F, W), BF), jax.ShapeDtypeStruct((F, W), BF)),
        in_specs=[vm] * 7, out_specs=(vm, vm), name="finish",
    )(parts[0], beside, arrived, own, t_own, ids, stat)

    score_rows = jnp.transpose(score, (1, 0, 2)).reshape(F, 16, 128)
    term_rows = jnp.transpose(terms.reshape(8, 8, 8, 128), (2, 0, 1, 3)).reshape(F, 8, 128)
    back = lax.all_to_all(
        jnp.concatenate([score_rows, term_rows], axis=1), "seq", split_axis=0, concat_axis=0, tiled=True)
    score_field = flip(back[:, :16].reshape(F, 2, W)).reshape(1, 128, W)
    frames = jnp.sum(back[:, 16:].astype(F32), axis=0).reshape(8, 2, F)
    frames = jnp.transpose(frames, (2, 1, 0)).reshape(F, 16)
    onehot = (ids == jnp.arange(CONCEPTS, dtype=jnp.int32)[None, :]).astype(F32)
    table_grad = jnp.dot(onehot.T, frames, precision=lax.Precision.HIGHEST)
    return (score_field, table_grad)


def solution(mesh):
    in_specs = (
        P("seq", None, "tp"),
        P("seq", None, "tp"),
        P("seq"),
        P(),
        P(None, "tp"),
        P(None, "tp"),
        P(None, "tp"),
    )
    out_specs = (P("seq", None, "tp"), P(None, ("seq", "tp")))
    return jax.shard_map(body, mesh=mesh, in_specs=in_specs, out_specs=out_specs, check_vma=False)
```

```python
import math

import jax
import jax.numpy as jnp
from jax import lax
from jax.experimental import pallas as pl
from jax.experimental.pallas import tpu as pltpu
from jax.sharding import PartitionSpec as P

D = 4096
HD = 128
CONCEPTS = 256
STEPS = 1000
EPS = 1e-06
F = 64
W = 1024
STEP = 40

BF = jnp.bfloat16
F32 = jnp.float32
NT = (((1,), (1,)), ((), ()))


def nt(a, b):
    return lax.dot_general(a, b, NT, preferred_element_type=F32)


def mod_kernel(t0, t1, t2, t3, ids_ref, steps_ref, mod_ref, late_ref, temp_ref):
    temp_ref[...] = jnp.zeros((F, 128), F32) + steps_ref[...]
    ids = ids_ref[:, 0:128].astype(F32)
    late_ref[...] = ids
    onehot = (ids[:, 0:1] == lax.broadcasted_iota(jnp.int32, (F, CONCEPTS), 1).astype(F32)).astype(BF)
    for k, table_ref in enumerate((t0, t1, t2, t3)):
        mod_ref[k] = 1.0 + jnp.dot(onehot, table_ref[...], preferred_element_type=F32)


def relay_kernel(*refs):
    v_ref, o_ref = refs[-2:]
    o_ref[...] = v_ref[...]


def pack_kernel(x_ref, d_ref, ids_ref, o_ref, in_s, out_s):
    y_hi = lax.axis_index("tp") >> 1
    for j in range(8):
        lanes = pl.ds(128 * j, 128)
        in_s[256 * j:256 * j + 128] = x_ref[:, lanes].astype(F32)
        in_s[256 * j + 128:256 * j + 256] = d_ref[:, lanes].astype(F32)
    for q in range(4):
        for j in range(8):
            rows = in_s[pl.ds(256 * j + (q // 2) * 128 + q % 2, F, stride=2), :]
            out_s[pl.ds(j * 4 + q, F, stride=STEP), :] = flip_rows(rows, y_hi)
        out_s[pl.ds(32 + q, F, stride=STEP), :] = jnp.zeros((F, 128), F32) + ids_ref[...].astype(F32)
    o_ref[...] = out_s[...].astype(BF)


def flip_rows(v, y_hi):
    v = v.reshape(8, 8, 128)
    swapped = jnp.concatenate([v[:, 4:8], v[:, 0:4]], axis=1)
    return jnp.where(y_hi == 1, swapped, v).reshape(F, 128)


def unpack_kernel(g_ref, x_ref, d_ref, ids_ref, in_s):
    in_s[...] = g_ref[...].astype(F32)
    for q in range(4):
        ref = (x_ref, d_ref)[q // 2]
        for j in range(8):
            ref[q % 2, :, 128 * j:128 * j + 128] = in_s[pl.ds(j * 4 + q, F, stride=STEP), :].astype(BF)
    ids_ref[:, 0:128] = in_s[pl.ds(32, F, stride=STEP), :].astype(BF)


def tail_kernel(g_ref, ids_ref, score_ref, table_ref, in_s, out_s):
    y_hi = lax.axis_index("tp") >> 1
    in_s[...] = g_ref[...].astype(F32)
    for p in range(2):
        for j in range(8):
            rows = in_s[pl.ds(p * 8 + j, F, stride=24), :]
            out_s[pl.ds(128 * j + p, F, stride=2), :] = flip_rows(rows, y_hi)
    for j in range(8):
        score_ref[:, 128 * j:128 * j + 128] = out_s[128 * j:128 * j + 128].astype(BF)
    total = jnp.sum(in_s[...].reshape(F, 24, 128)[:, 16:24], axis=0)
    cols = jnp.concatenate([total[:, 0:64], total[:, 64:128]], axis=0)
    ids = ids_ref[:, 0:1]
    onehot = (ids == lax.broadcasted_iota(jnp.int32, (F, CONCEPTS), 1).astype(F32)).astype(F32)
    table_ref[...] = jnp.dot(cols, onehot, precision=lax.Precision.HIGHEST, preferred_element_type=F32)


def forward(h_s, w_ref, out_ref):
    for part in range(4):
        cols = pl.ds(256 * part, 256)
        total = jnp.zeros((2 * F, 256), F32)
        for k in range(4):
            total = total + jnp.dot(h_s[k], w_ref[k, :, cols], preferred_element_type=F32)
        out_ref[:, cols] = total.astype(BF)


def eye128():
    return lax.broadcasted_iota(jnp.int32, (128, 128), 0) == lax.broadcasted_iota(jnp.int32, (128, 128), 1)


def spots():
    return [(pl.ds(64 * p, 64), pl.ds(128 * h, 128), pl.ds(512 + 128 * h, 128)) for p in range(2) for h in range(4)]


def latent_kernel(wq_ref, wk_ref, x0, x1, x2, x3, mod_ref, temp_ref,
                  u0, u1, u2, u3, qk_ref, soft_ref, stat_ref, w_ref, h_s, g_s, sems):
    xs, outs = (x0, x1, x2, x3), (u0, u1, u2, u3)
    me = lax.axis_index("tp")
    copies = []
    for k in range(4):
        rows = pl.ds(pl.multiple_of((me ^ k) * W, W), W)
        copies.append([
            pltpu.make_async_copy(ref.at[rows], w_ref.at[k, :, pl.ds(512 * i, 512)], sems.at[2 * k + i])
            for i, ref in enumerate((wq_ref, wk_ref))])
        for copy in copies[k]:
            copy.start()
    sq = jnp.zeros((2 * F, 128), F32)
    for k in range(4):
        for j in range(8):
            x = xs[k][:, :, 128 * j:128 * j + 128].astype(F32).reshape(2 * F, 128)
            sq = sq + x * x
    inv = lax.rsqrt(jnp.sum(sq, axis=-1, keepdims=True) / D + EPS)
    lane = lax.broadcasted_iota(jnp.int32, (2 * F, 128), 1)
    stat_ref[...] = jnp.where(lane == 0, inv, 0.0)
    for k in range(4):
        for j in range(4):
            lanes = pl.ds(256 * j, 256)
            m = mod_ref[k, :, lanes]
            n = xs[k][:, :, lanes].astype(F32).reshape(2 * F, 256) * inv
            h_s[k, :, lanes] = (n * jnp.concatenate([m, m], axis=0)).astype(BF)
    total = jnp.zeros((2 * F, W), F32)
    for k in range(4):
        for copy in copies[k]:
            copy.wait()
        total = total + jnp.dot(h_s[k], w_ref[k], preferred_element_type=F32)
    qk_ref[...] = total.astype(BF)

    temp = temp_ref[:, 0:64]
    where = spots()
    qs = [qk_ref[r, ql] for r, ql, _ in where]
    ks = [qk_ref[r, kl] for r, _, kl in where]
    scores = [nt(q, k) * temp for q, k in zip(qs, ks)]
    tops = [jnp.max(v, axis=-1, keepdims=True) for v in scores]
    exps = [jnp.exp(v - t) for v, t in zip(scores, tops)]
    sums = [jnp.sum(e, axis=-1, keepdims=True) for e in exps]
    ws = [e / v for e, v in zip(exps, sums)]
    for i, w in enumerate(ws):
        soft_ref[64 * i:64 * i + 64, :] = w
    gqs = [(-jnp.dot(w.astype(BF), k, preferred_element_type=F32)).astype(BF) for w, k in zip(ws, ks)]
    gks = [(-jnp.dot(w.T.astype(BF), q, preferred_element_type=F32)).astype(BF) for w, q in zip(ws, qs)]
    part = [jnp.zeros((F, HD), F32), jnp.zeros((F, HD), F32)]
    for i, (r, ql, kl) in enumerate(where):
        g_s[r, ql] = gqs[i]
        g_s[r, kl] = gks[i]
        part[i // 4] = part[i // 4] + gqs[i].astype(F32) * qs[i].astype(F32) + gks[i].astype(F32) * ks[i].astype(F32)
    scal = jnp.sum(jnp.concatenate(part, axis=0), axis=-1, keepdims=True)
    srow = jnp.sum(jnp.where(eye128(), scal, 0.0), axis=0, keepdims=True)
    hi = srow.astype(BF).astype(F32)
    sub = lax.broadcasted_iota(jnp.int32, (16, 128), 0)
    stats = jnp.where(sub == 0, hi, jnp.where(sub == 1, srow - hi, 0.0)).astype(BF)
    for k in (3, 2, 1, 0):
        for j in range(4):
            outs[k][0:128, 256 * j:256 * j + 256] = nt(g_s[...], w_ref[k, 256 * j:256 * j + 256, :]).astype(BF)
        outs[k][128:144, 0:128] = stats
        outs[k][128:144, 128:1024] = jnp.zeros((16, 896), BF)


def normed_of(x_ref, d_ref, lanes, inv, mean):
    n = x_ref[:, :, lanes].astype(F32).reshape(2 * F, -1) * inv
    d = d_ref[:, :, lanes].astype(F32).reshape(2 * F, -1)
    return n, inv * (d - n * mean)


def tangent_kernel(x0, x1, x2, x3, d0, d1, d2, d3, u0, u1, u2, u3, mod_ref, stat_ref, qk_ref, soft_ref, temp_ref, _, w_ref,
                   o0, o1, o2, o3, h_s, tan_s, g_s, drift_s, term_s):
    xs, ds, us, outs = (x0, x1, x2, x3), (d0, d1, d2, d3), (u0, u1, u2, u3), (o0, o1, o2, o3)
    me = lax.axis_index("tp")
    sd = jnp.zeros((2 * F, 128), F32)
    for k in range(4):
        for j in range(8):
            x = xs[k][:, :, 128 * j:128 * j + 128].astype(F32).reshape(2 * F, 128)
            d = ds[k][:, :, 128 * j:128 * j + 128].astype(F32).reshape(2 * F, 128)
            sd = sd + x * d
    inv = jnp.sum(stat_ref[...], axis=-1, keepdims=True)
    mean = inv * (jnp.sum(sd, axis=-1, keepdims=True) / D)

    for k in range(4):
        for j in range(4):
            lanes = pl.ds(256 * j, 256)
            nd = normed_of(xs[k], ds[k], lanes, inv, mean)[1]
            m = mod_ref[k, :, lanes]
            h_s[k, :, lanes] = (nd * jnp.concatenate([m, m], axis=0)).astype(BF)
    forward(h_s, w_ref, tan_s)

    temp = temp_ref[:, 0:64]
    where = spots()
    qs = [qk_ref[r, ql] for r, ql, _ in where]
    ks = [qk_ref[r, kl] for r, _, kl in where]
    qts = [tan_s[r, ql] for r, ql, _ in where]
    kts = [tan_s[r, kl] for r, _, kl in where]
    ws = [soft_ref[64 * i:64 * i + 64, :] for i in range(8)]
    tdots = [nt(jnp.concatenate([a, b], axis=1), jnp.concatenate([c, d], axis=1)) for a, b, c, d in zip(qts, qs, ks, kts)]
    means = [jnp.sum(w * t, axis=-1, keepdims=True) for w, t in zip(ws, tdots)]
    curs = [temp * w * (t - m) for w, t, m in zip(ws, tdots, means)]
    cw = [jnp.concatenate([c, w], axis=1).astype(BF) for w, c in zip(ws, curs)]
    cwt = [jnp.concatenate([c, w], axis=0).T.astype(BF) for w, c in zip(ws, curs)]
    aqs = [jnp.dot(m, jnp.concatenate([k, kt], axis=0), preferred_element_type=F32) for m, k, kt in zip(cw, ks, kts)]
    aks = [jnp.dot(m, jnp.concatenate([q, qt], axis=0), preferred_element_type=F32) for m, q, qt in zip(cwt, qs, qts)]
    for i, (r, ql, kl) in enumerate(where):
        g_s[r, ql] = (-aqs[i]).astype(BF)
        g_s[r, kl] = (-aks[i]).astype(BF)

    for k in range(4):
        for j in range(4):
            drift_s[k, :, 256 * j:256 * j + 256] = nt(g_s[...], w_ref[k, 256 * j:256 * j + 256, :])
    rr = lax.broadcasted_iota(jnp.int32, (128, 256), 0)
    cc = lax.broadcasted_iota(jnp.int32, (128, 256), 1)
    pick = (((rr >> 3) & 3) == (cc >> 6)) & ((rr >> 5) == ((cc >> 4) & 3)) & ((rr & 7) == (cc & 7))
    pick = pick.astype(BF)
    late = ((lax.broadcasted_iota(jnp.int32, (F, 256), 1) >> 3) & 1) == 1
    for k in range(4):
        for j in range(4):
            lanes = pl.ds(256 * j, 256)
            n, nd = normed_of(xs[k], ds[k], lanes, inv, mean)
            terms = n * drift_s[k, :, lanes] + nd * us[k][0:128, lanes].astype(F32)
            terms = terms[0:64] + terms[64:128]
            split = jnp.concatenate([jnp.where(late, 0.0, terms), jnp.where(late, terms, 0.0)], axis=0).astype(BF)
            moved = nt(pick, split).astype(BF)
            spot = pl.ds(pl.multiple_of((me ^ k) * 256 + 128 * (j // 2), 128), 128)
            low = 32 * (j % 2)
            for t in range(4):
                term_s[t, low:low + 32, spot] = moved[32 * t:32 * t + 32]
    for k in range(4):
        outs[k][...] = term_s[me ^ k]


def local_call(kernel, args, outs, scratch, limit, name, flops=1 << 20, hbm=0):
    vm = pl.BlockSpec(memory_space=pltpu.VMEM)
    args = [pltpu.with_memory_space_constraint(v, pltpu.HBM) if i < hbm else v for i, v in enumerate(args)]
    return pl.pallas_call(
        kernel,
        out_shape=tuple(jax.ShapeDtypeStruct(s, t) for s, t in outs),
        in_specs=[pl.BlockSpec(memory_space=pltpu.HBM)] * hbm + [vm] * (len(args) - hbm),
        out_specs=tuple(vm for _ in outs),
        scratch_shapes=scratch,
        compiler_params=pltpu.CompilerParams(vmem_limit_bytes=limit * 1024 * 1024),
        cost_estimate=pl.CostEstimate(flops=flops, bytes_accessed=1 << 20, transcendentals=0),
        name=name,
    )(*args)


def add_kernel(_, a_ref, b_ref, o_ref):
    o_ref[...] = (a_ref[...].astype(F32) + b_ref[...].astype(F32)).astype(BF)


def merge_kernel(a_ref, b_ref, o_ref):
    o_ref[0:128, :] = (a_ref[0:128, :].astype(F32) + b_ref[0:128, :].astype(F32)).astype(BF)
    o_ref[128:144, :] = jnp.concatenate(
        [a_ref[128:144, 0:128], b_ref[128:144, 0:128], a_ref[128:144, 256:1024]], axis=1)


def score_kernel(a_ref, b_ref, c_ref, x_ref, mod_ref, stat_ref, score_ref):
    srow = jnp.zeros((1, 128), F32)
    for ref, lane in ((a_ref, 0), (b_ref, 0), (c_ref, 0), (c_ref, 128)):
        part = ref[128:144, lane:lane + 128].astype(F32)
        srow = srow + (part[0:1] + part[1:2])
    mean = jnp.sum(jnp.where(eye128(), srow, 0.0), axis=1, keepdims=True) / D
    inv = jnp.sum(stat_ref[...], axis=1, keepdims=True)
    for j in range(4):
        lanes = pl.ds(256 * j, 256)
        units = (a_ref[0:128, lanes].astype(F32) + b_ref[0:128, lanes].astype(F32)) + c_ref[0:128, lanes].astype(F32)
        mod = mod_ref[0, :, lanes]
        mod = jnp.concatenate([mod, mod], axis=0)
        x = x_ref[:, :, lanes].astype(F32).reshape(2 * F, 256)
        score_ref[:, :, lanes] = (inv * (mod * units - (x * inv) * mean)).astype(BF).reshape(2, F, 256)


def body(latent, direction, concept, timestep, concept_table, w_query, w_key):
    cross = []
    for s in range(64):
        for t in range(4):
            cross.append((4 * s + t, 4 * (s ^ 4) + (t ^ 2)))
    core = [(t, t ^ 1) for t in range(4)]
    swap_core = lambda v: lax.ppermute(v, "tp", core)
    swap_chip = lambda v: lax.ppermute(v, ("seq", "tp"), cross)
    vmem = pltpu.VMEM

    sent, = local_call(
        pack_kernel, (latent.reshape(2 * F, W), direction.reshape(2 * F, W), concept.reshape(1, 1)),
        (((F * STEP, 128), BF),), (vmem((4 * F * 8, 128), F32), vmem((F * STEP, 128), F32)), 60, "pack")
    got = lax.all_to_all(sent, "seq", split_axis=0, concat_axis=0, tiled=True)

    t_core = swap_core(concept_table)
    t_chip = swap_chip(concept_table)
    t_both = swap_core(t_chip)

    half = ((2, F, W), BF)
    x0, d0, ids = local_call(
        unpack_kernel, (got,), (half, half, ((F, 2 * W), BF)), (vmem((F * STEP, 128), F32),), 8, "unpack")

    steps = ((0.25 + 1.75 * timestep.astype(F32) / STEPS) / math.sqrt(HD)).reshape(F, 1)
    mod, ids_late, temp = local_call(
        mod_kernel, (concept_table, t_core, t_chip, t_both, ids, steps),
        (((4, F, W), F32), ((F, 128), F32), ((F, 128), F32)), (), 8, "mod", 1 << 30)
    relay = lambda *v: local_call(relay_kernel, v, (half,), (), 4, "relay")[0]
    x2 = swap_chip(x0)
    x1 = swap_core(x0)
    x3 = swap_core(x2)
    d1 = swap_core(d0)
    d2 = swap_chip(relay(x3, mod, d0))

    units, terms = ((144, W), BF), ((F, W), BF)
    u0, u1, u2, u3, qk, soft, stat, weights = local_call(
        latent_kernel, (w_query, w_key, x0, x1, x2, x3, mod, temp),
        (units,) * 4
        + (((2 * F, W), BF), ((8 * F, F), F32), ((2 * F, 128), F32), ((4, W, W), BF)),
        (vmem((4, 2 * F, W), BF), vmem((2 * F, W), BF), pltpu.SemaphoreType.DMA((8,))), 20, "latents", 1 << 30, hbm=2)
    d3 = swap_core(relay(stat, d2))
    far = swap_core(u3)
    summed, = local_call(merge_kernel, (u2, far), (units,), (), 4, "merge")
    arrived = swap_chip(summed)
    beside = swap_core(u1)

    v0, v1, v2, v3 = local_call(
        tangent_kernel,
        (x0, x1, x2, x3, d0, d1, d2, d3, u0, u1, u2, u3, mod, stat, qk, soft, temp, summed, weights), (terms,) * 4,
        (vmem((4, 2 * F, W), BF), vmem((2 * F, W), BF), vmem((2 * F, W), BF), vmem((4, 2 * F, W), F32),
         vmem((4, F, W), BF)), 20, "tangent", 1 << 34)
    score, = local_call(score_kernel, (u0, beside, arrived, x0, mod, stat), (half,), (), 4, "score")
    v_far = swap_core(v3)
    v_sum, = local_call(add_kernel, (score, v2, v_far), (terms,), (), 4, "add")
    v_chip = swap_chip(v_sum)
    v_near = swap_core(v1)
    total = (v0.astype(F32) + v_near.astype(F32) + v_chip.astype(F32)).astype(BF)

    score_rows = jnp.transpose(score, (1, 0, 2)).reshape(F, 16, 128)
    term_rows = jnp.transpose(total.reshape(8, 8, 8, 128), (2, 0, 1, 3)).reshape(F, 8, 128)
    back = lax.all_to_all(
        jnp.concatenate([score_rows, term_rows], axis=1), "seq", split_axis=0, concat_axis=0, tiled=True)
    score_field, table = local_call(
        tail_kernel, (back.reshape(F * 24, 128), ids_late), (((2 * F, W), BF), ((16, CONCEPTS), F32)),
        (vmem((F * 24, 128), F32), vmem((2 * F * 8, 128), F32)), 8, "tail")
    return (score_field.reshape(1, 2 * F, W), table.T)


def solution(mesh):
    in_specs = (
        P("seq", None, "tp"),
        P("seq", None, "tp"),
        P("seq"),
        P(),
        P(None, "tp"),
        P(None, "tp"),
        P(None, "tp"),
    )
    out_specs = (P("seq", None, "tp"), P(None, ("seq", "tp")))
    return jax.shard_map(body, mesh=mesh, in_specs=in_specs, out_specs=out_specs, check_vma=False)
```

```python
import math

import jax
import jax.numpy as jnp
from jax import lax
from jax.experimental import pallas as pl
from jax.experimental.pallas import tpu as pltpu
from jax.sharding import PartitionSpec as P

D = 4096
HD = 128
CONCEPTS = 256
STEPS = 1000
EPS = 1e-06
F = 64
W = 1024
STEP = 36

BF = jnp.bfloat16
F32 = jnp.float32
NT = (((1,), (1,)), ((), ()))


def nt(a, b):
    return lax.dot_general(a, b, NT, preferred_element_type=F32)


def turn_kernel(wq_ref, wk_ref, o_ref, token_ref, w_s, t_s, sems, out_sems):
    me = lax.axis_index("tp")
    copies, outs = [], []
    for k in range(4):
        rows = pl.ds(pl.multiple_of((me ^ k) * W, W), W)
        for i, ref in enumerate((wq_ref, wk_ref)):
            copy = pltpu.make_async_copy(ref.at[rows], w_s.at[k, :, pl.ds(512 * i, 512)], sems.at[2 * k + i])
            copy.start()
            copies.append(copy)
    for k in range(4):
        copies[2 * k].wait()
        copies[2 * k + 1].wait()
        for j in range(4):
            t_s[k, :, 256 * j:256 * j + 256] = w_s[k, 256 * j:256 * j + 256, :].T
        out = pltpu.make_async_copy(t_s.at[k], o_ref.at[k], out_sems.at[k])
        out.start()
        outs.append(out)
    for out in outs:
        out.wait()
    token_ref[...] = jnp.zeros_like(token_ref)


def prepare_kernel(wq_ref, wk_ref, table_ref, t1, t2, t3, ids_ref, steps_ref, w_ref, mod_ref, t0, sems):
    me = lax.axis_index("tp")
    own = pltpu.make_async_copy(table_ref, t0, sems.at[8])
    own.start()
    copies = []
    for k in range(4):
        rows = pl.ds(pl.multiple_of((me ^ k) * W, W), W)
        for i, ref in enumerate((wq_ref, wk_ref)):
            copy = pltpu.make_async_copy(ref.at[rows], w_ref.at[k, :, pl.ds(512 * i, 512)], sems.at[2 * k + i])
            copy.start()
            copies.append(copy)
    ids = ids_ref[:, 0:128].astype(F32)
    onehot = (ids[:, 0:1] == lax.broadcasted_iota(jnp.int32, (F, CONCEPTS), 1).astype(F32)).astype(BF)
    for k, ref in ((1, t1), (2, t2), (3, t3), (0, t0)):
        if k == 0:
            own.wait()
        mod_ref[k] = 1.0 + jnp.dot(onehot, ref[...], preferred_element_type=F32)
    mod_ref[4, :, 0:128] = ids
    mod_ref[4, :, 128:256] = jnp.zeros((F, 128), F32) + steps_ref[...]
    for copy in copies:
        copy.wait()


def relay_kernel(_, v_ref, o_ref):
    o_ref[...] = v_ref[...]


def join_kernel(_, a_ref, b_ref, o_ref):
    o_ref[0:2] = a_ref[...]
    o_ref[2:4] = b_ref[...]


def slices(own, chip, near):
    return [own.at[0:2], near.at[0:2], chip.at[0:2], near.at[2:4]]


def pack_kernel(x_ref, d_ref, ids_ref, o_ref, in_s, out_s):
    y_hi = lax.axis_index("tp") >> 1
    for j in range(8):
        lanes = pl.ds(128 * j, 128)
        in_s[256 * j:256 * j + 128] = x_ref[:, lanes].astype(F32)
        in_s[256 * j + 128:256 * j + 256] = d_ref[:, lanes].astype(F32)
    for q in range(4):
        for j in range(8):
            rows = in_s[pl.ds(256 * j + (q // 2) * 128 + q % 2, F, stride=2), :]
            out_s[pl.ds(j * 4 + q, F, stride=STEP), :] = flip_rows(rows, y_hi)
        out_s[pl.ds(32 + q, F, stride=STEP), :] = jnp.zeros((F, 128), F32) + ids_ref[0].astype(F32)
    o_ref[...] = out_s[...].astype(BF).reshape(F, 9, 4, 128)


def flip_rows(v, y_hi):
    v = v.reshape(8, 8, 128)
    swapped = jnp.concatenate([v[:, 4:8], v[:, 0:4]], axis=1)
    return jnp.where(y_hi == 1, swapped, v).reshape(F, 128)


def unpack_kernel(_, g_ref, x_ref, d_ref, ids_ref, in_s):
    in_s[...] = g_ref[...].reshape(F * STEP, 128).astype(F32)
    for q in range(4):
        ref = (x_ref, d_ref)[q // 2]
        for j in range(8):
            ref[q % 2, :, 128 * j:128 * j + 128] = in_s[pl.ds(j * 4 + q, F, stride=STEP), :].astype(BF)
    ids_ref[:, 0:128] = in_s[pl.ds(32, F, stride=STEP), :].astype(BF)


def tail_kernel(g_ref, ids_ref, score_ref, table_ref, in_s, out_s):
    y_hi = lax.axis_index("tp") >> 1
    in_s[...] = g_ref[...].astype(F32)
    for p in range(2):
        for j in range(8):
            rows = in_s[pl.ds(p * 8 + j, F, stride=24), :]
            out_s[pl.ds(128 * j + p, F, stride=2), :] = flip_rows(rows, y_hi)
    for j in range(8):
        score_ref[:, 128 * j:128 * j + 128] = out_s[128 * j:128 * j + 128].astype(BF)
    total = jnp.sum(in_s[...].reshape(F, 24, 128)[:, 16:24], axis=0)
    cols = jnp.concatenate([total[:, 0:64], total[:, 64:128]], axis=0)
    ids = ids_ref[:, 0:1]
    onehot = (ids == lax.broadcasted_iota(jnp.int32, (F, CONCEPTS), 1).astype(F32)).astype(F32)
    table_ref[...] = jnp.dot(cols, onehot, precision=lax.Precision.HIGHEST, preferred_element_type=F32)


def forward(h_s, w_ref, out_ref):
    for part in range(4):
        cols = pl.ds(256 * part, 256)
        total = jnp.zeros((2 * F, 256), F32)
        for k in range(4):
            total = total + jnp.dot(h_s[k], w_ref[k, :, cols], preferred_element_type=F32)
        out_ref[:, cols] = total.astype(BF)


def eye128():
    return lax.broadcasted_iota(jnp.int32, (128, 128), 0) == lax.broadcasted_iota(jnp.int32, (128, 128), 1)


def spots():
    return [(pl.ds(64 * p, 64), pl.ds(128 * h, 128), pl.ds(512 + 128 * h, 128)) for p in range(2) for h in range(4)]


def latent_kernel(turned_ref, x0, x2, xn, mod_ref, _, w_ref,
                  u0, u1, u2, u3_low, u3_high, qk_ref, soft_ref, stat_ref, back_ref, h_s, g_s, u3, sems):
    xs, outs = slices(x0, x2, xn), (u0, u1, u2, u3)
    copies = [pltpu.make_async_copy(turned_ref.at[k], back_ref.at[k], sems.at[k]) for k in range(4)]
    for k in (3, 2, 1, 0):
        copies[k].start()
    sq = jnp.zeros((2 * F, 128), F32)
    for k in range(4):
        for j in range(8):
            x = xs[k][:, :, 128 * j:128 * j + 128].astype(F32).reshape(2 * F, 128)
            sq = sq + x * x
    inv = lax.rsqrt(jnp.sum(sq, axis=-1, keepdims=True) / D + EPS)
    lane = lax.broadcasted_iota(jnp.int32, (2 * F, 128), 1)
    stat_ref[...] = jnp.where(lane == 0, inv, 0.0)
    for k in range(4):
        for j in range(4):
            lanes = pl.ds(256 * j, 256)
            m = mod_ref[k, :, lanes]
            n = xs[k][:, :, lanes].astype(F32).reshape(2 * F, 256) * inv
            h_s[k, :, lanes] = (n * jnp.concatenate([m, m], axis=0)).astype(BF)
    forward(h_s, w_ref, qk_ref)

    temp = mod_ref[4, :, 128:192]
    where = spots()
    qs = [qk_ref[r, ql] for r, ql, _ in where]
    ks = [qk_ref[r, kl] for r, _, kl in where]
    scores = [nt(q, k) * temp for q, k in zip(qs, ks)]
    tops = [jnp.max(v, axis=-1, keepdims=True) for v in scores]
    exps = [jnp.exp(v - t) for v, t in zip(scores, tops)]
    sums = [jnp.sum(e, axis=-1, keepdims=True) for e in exps]
    ws = [e / v for e, v in zip(exps, sums)]
    for i, w in enumerate(ws):
        soft_ref[64 * i:64 * i + 64, :] = w
    gqs = [(-jnp.dot(w.astype(BF), k, preferred_element_type=F32)).astype(BF) for w, k in zip(ws, ks)]
    gks = [(-jnp.dot(w.T.astype(BF), q, preferred_element_type=F32)).astype(BF) for w, q in zip(ws, qs)]
    part = [jnp.zeros((F, HD), F32), jnp.zeros((F, HD), F32)]
    for i, (r, ql, kl) in enumerate(where):
        g_s[r, ql] = gqs[i]
        g_s[r, kl] = gks[i]
        part[i // 4] = part[i // 4] + gqs[i].astype(F32) * qs[i].astype(F32) + gks[i].astype(F32) * ks[i].astype(F32)
    scal = jnp.sum(jnp.concatenate(part, axis=0), axis=-1, keepdims=True)
    srow = jnp.sum(jnp.where(eye128(), scal, 0.0), axis=0, keepdims=True)
    hi = srow.astype(BF).astype(F32)
    sub = lax.broadcasted_iota(jnp.int32, (16, 128), 0)
    stats = jnp.where(sub == 0, hi, jnp.where(sub == 1, srow - hi, 0.0)).astype(BF)
    for k in (3, 2, 1, 0):
        copies[k].wait()
        for j in range(4):
            lanes = pl.ds(256 * j, 256)
            outs[k][0:128, lanes] = jnp.dot(g_s[...], back_ref[k, :, lanes], preferred_element_type=F32).astype(BF)
        outs[k][128:144, 0:128] = stats
        outs[k][128:144, 128:1024] = jnp.zeros((16, 896), BF)
    u3_low[...] = u3[0:64, :]
    u3_high[...] = u3[64:144, :]


def normed_of(x_ref, d_ref, lanes, inv, mean):
    n = x_ref[:, :, lanes].astype(F32).reshape(2 * F, -1) * inv
    d = d_ref[:, :, lanes].astype(F32).reshape(2 * F, -1)
    return n, inv * (d - n * mean)


def tangent_kernel(x0, x2, xn, d0, d2, dn, u0, u1, u2, u3_low, u3_high, mod_ref, stat_ref, qk_ref, soft_ref, _, w_ref, back_ref,
                   o0, o2, near_ref, ids_ref, h_s, tan_s, g_s, drift_s, term_s):
    xs, ds = slices(x0, x2, xn), slices(d0, d2, dn)
    me = lax.axis_index("tp")
    ids_ref[...] = mod_ref[4, :, 0:128]
    sd = jnp.zeros((2 * F, 128), F32)
    for k in range(4):
        for j in range(8):
            x = xs[k][:, :, 128 * j:128 * j + 128].astype(F32).reshape(2 * F, 128)
            d = ds[k][:, :, 128 * j:128 * j + 128].astype(F32).reshape(2 * F, 128)
            sd = sd + x * d
    inv = jnp.sum(stat_ref[...], axis=-1, keepdims=True)
    mean = inv * (jnp.sum(sd, axis=-1, keepdims=True) / D)

    for k in range(4):
        for j in range(4):
            lanes = pl.ds(256 * j, 256)
            nd = normed_of(xs[k], ds[k], lanes, inv, mean)[1]
            m = mod_ref[k, :, lanes]
            h_s[k, :, lanes] = (nd * jnp.concatenate([m, m], axis=0)).astype(BF)
    forward(h_s, w_ref, tan_s)

    temp = mod_ref[4, :, 128:192]
    where = spots()
    qs = [qk_ref[r, ql] for r, ql, _ in where]
    ks = [qk_ref[r, kl] for r, _, kl in where]
    qts = [tan_s[r, ql] for r, ql, _ in where]
    kts = [tan_s[r, kl] for r, _, kl in where]
    ws = [soft_ref[64 * i:64 * i + 64, :] for i in range(8)]
    tdots = [nt(jnp.concatenate([a, b], axis=1), jnp.concatenate([c, d], axis=1)) for a, b, c, d in zip(qts, qs, ks, kts)]
    means = [jnp.sum(w * t, axis=-1, keepdims=True) for w, t in zip(ws, tdots)]
    curs = [temp * w * (t - m) for w, t, m in zip(ws, tdots, means)]
    cw = [jnp.concatenate([c, w], axis=1).astype(BF) for w, c in zip(ws, curs)]
    cwt = [jnp.concatenate([c, w], axis=0).T.astype(BF) for w, c in zip(ws, curs)]
    aqs = [jnp.dot(m, jnp.concatenate([k, kt], axis=0), preferred_element_type=F32) for m, k, kt in zip(cw, ks, kts)]
    aks = [jnp.dot(m, jnp.concatenate([q, qt], axis=0), preferred_element_type=F32) for m, q, qt in zip(cwt, qs, qts)]
    for i, (r, ql, kl) in enumerate(where):
        g_s[r, ql] = (-aqs[i]).astype(BF)
        g_s[r, kl] = (-aks[i]).astype(BF)

    for k in range(4):
        for j in range(4):
            lanes = pl.ds(256 * j, 256)
            drift_s[k, :, lanes] = jnp.dot(g_s[...], back_ref[k, :, lanes], preferred_element_type=F32)
    rr = lax.broadcasted_iota(jnp.int32, (128, 256), 0)
    cc = lax.broadcasted_iota(jnp.int32, (128, 256), 1)
    pick = (((rr >> 3) & 3) == (cc >> 6)) & ((rr >> 5) == ((cc >> 4) & 3)) & ((rr & 7) == (cc & 7))
    pick = pick.astype(BF)
    late = ((lax.broadcasted_iota(jnp.int32, (F, 256), 1) >> 3) & 1) == 1
    for k in range(4):
        for j in range(4):
            lanes = pl.ds(256 * j, 256)
            n, nd = normed_of(xs[k], ds[k], lanes, inv, mean)
            if k == 3:
                units = jnp.concatenate([u3_low[:, lanes], u3_high[0:64, lanes]], axis=0)
            else:
                units = (u0, u1, u2)[k][0:128, lanes]
            terms = n * drift_s[k, :, lanes] + nd * units.astype(F32)
            terms = terms[0:64] + terms[64:128]
            split = jnp.concatenate([jnp.where(late, 0.0, terms), jnp.where(late, terms, 0.0)], axis=0).astype(BF)
            moved = nt(pick, split).astype(BF)
            spot = pl.ds(pl.multiple_of((me ^ k) * 256 + 128 * (j // 2), 128), 128)
            low = 32 * (j % 2)
            for t in range(4):
                term_s[t, low:low + 32, spot] = moved[32 * t:32 * t + 32]
    o0[...] = term_s[me]
    o2[...] = term_s[me ^ 2]
    near_ref[0:64, :] = term_s[me ^ 3]
    near_ref[64:128, :] = term_s[me ^ 1]


def local_call(kernel, args, outs, scratch, limit, name, flops=1 << 20, hbm=0, smem=0):
    vm = pl.BlockSpec(memory_space=pltpu.VMEM)
    args = [pltpu.with_memory_space_constraint(v, pltpu.HBM) if i < hbm else v for i, v in enumerate(args)]
    return pl.pallas_call(
        kernel,
        out_shape=tuple(jax.ShapeDtypeStruct(s, t) for s, t in outs),
        in_specs=[pl.BlockSpec(memory_space=pltpu.HBM)] * hbm + [vm] * (len(args) - hbm - smem)
        + [pl.BlockSpec(memory_space=pltpu.SMEM)] * smem,
        out_specs=tuple(vm for _ in outs),
        scratch_shapes=scratch,
        compiler_params=pltpu.CompilerParams(vmem_limit_bytes=limit * 1024 * 1024),
        cost_estimate=pl.CostEstimate(flops=flops, bytes_accessed=1 << 20, transcendentals=0),
        name=name,
    )(*args)


def add_kernel(_, a_ref, b_ref, o_ref):
    o_ref[...] = (a_ref[...].astype(F32) + b_ref[0:64, :].astype(F32)).astype(BF)


def merge_kernel(a_ref, low_ref, high_ref, o_ref):
    o_ref[0:64, :] = (a_ref[0:64, :].astype(F32) + low_ref[...].astype(F32)).astype(BF)
    o_ref[64:128, :] = (a_ref[64:128, :].astype(F32) + high_ref[0:64, :].astype(F32)).astype(BF)
    o_ref[128:144, :] = jnp.concatenate(
        [a_ref[128:144, 0:128], high_ref[64:80, 0:128], a_ref[128:144, 256:1024]], axis=1)


def score_kernel(a_ref, b_ref, c_ref, x_ref, mod_ref, stat_ref, score_ref, out_s):
    srow = jnp.zeros((1, 128), F32)
    for ref, lane in ((a_ref, 0), (b_ref, 0), (c_ref, 0), (c_ref, 128)):
        part = ref[128:144, lane:lane + 128].astype(F32)
        srow = srow + (part[0:1] + part[1:2])
    mean = jnp.sum(jnp.where(eye128(), srow, 0.0), axis=1, keepdims=True) / D
    inv = jnp.sum(stat_ref[...], axis=1, keepdims=True)
    for j in range(4):
        lanes = pl.ds(256 * j, 256)
        units = (a_ref[0:128, lanes].astype(F32) + b_ref[0:128, lanes].astype(F32)) + c_ref[0:128, lanes].astype(F32)
        mod = mod_ref[0, :, lanes]
        mod = jnp.concatenate([mod, mod], axis=0)
        x = x_ref[:, :, lanes].astype(F32).reshape(2 * F, 256)
        score = inv * (mod * units - (x * inv) * mean)
        for p in range(2):
            for i in range(2):
                out_s[pl.ds(8 * p + 2 * j + i, F, stride=16), :] = score[64 * p:64 * p + 64, 128 * i:128 * i + 128]
    score_ref[...] = out_s[...].astype(BF)


def finish_kernel(score_ref, a_ref, b_ref, c_ref, o_ref, out_s):
    out_s[:, 0:16] = score_ref[...].astype(F32).reshape(F, 16, 128)
    total = (a_ref[...].astype(F32) + b_ref[64:128, :].astype(F32)) + c_ref[...].astype(F32)
    for j in range(8):
        out_s[8 * j:8 * j + 8, 16:24] = total[:, 128 * j:128 * j + 128].reshape(8, 8, 128)
    o_ref[...] = out_s[...].reshape(F * 24, 128).astype(BF)


def body(latent, direction, concept, timestep, concept_table, w_query, w_key):
    cross = []
    for s in range(64):
        for t in range(4):
            cross.append((4 * s + t, 4 * (s ^ 4) + (t ^ 2)))
    core = [(t, t ^ 1) for t in range(4)]
    swap_core = lambda v: lax.ppermute(v, "tp", core)
    swap_chip = lambda v: lax.ppermute(v, ("seq", "tp"), cross)
    vmem = pltpu.VMEM

    sent, = local_call(
        pack_kernel, (latent.reshape(2 * F, W), direction.reshape(2 * F, W), concept),
        (((F, 9, 4, 128), BF),), (vmem((4 * F * 8, 128), F32), vmem((F * STEP, 128), F32)), 60, "pack", smem=1)
    got = lax.all_to_all(sent, "seq", split_axis=0, concat_axis=0, tiled=True)

    hbm = pl.BlockSpec(memory_space=pltpu.HBM)
    turned, token = pl.pallas_call(
        turn_kernel,
        out_shape=(jax.ShapeDtypeStruct((4, W, W), BF), jax.ShapeDtypeStruct((8, 128), F32)),
        in_specs=[hbm, hbm],
        out_specs=(hbm, pl.BlockSpec(memory_space=pltpu.VMEM)),
        scratch_shapes=[vmem((4, W, W), BF), vmem((4, W, W), BF),
                        pltpu.SemaphoreType.DMA((8,)), pltpu.SemaphoreType.DMA((4,))],
        compiler_params=pltpu.CompilerParams(vmem_limit_bytes=24 * 1024 * 1024),
        cost_estimate=pl.CostEstimate(flops=1 << 33, bytes_accessed=1 << 24, transcendentals=0),
        name="turn",
    )(pltpu.with_memory_space_constraint(w_query, pltpu.HBM), pltpu.with_memory_space_constraint(w_key, pltpu.HBM))
    t_core = swap_core(concept_table)
    t_chip = swap_chip(concept_table)
    t_both = swap_core(t_chip)

    half = ((2, F, W), BF)
    x0, d0, ids = local_call(
        unpack_kernel, (token, got), (half, half, ((F, 2 * W), BF)), (vmem((F * STEP, 128), F32),), 8, "unpack")

    steps = ((0.25 + 1.75 * timestep.astype(F32) / STEPS) / math.sqrt(HD)).reshape(F, 1)
    weights, mod = local_call(
        prepare_kernel, (w_query, w_key, concept_table, t_core, t_chip, t_both, ids, steps),
        (((4, W, W), BF), ((5, F, W), F32)), (vmem((CONCEPTS, W), BF), pltpu.SemaphoreType.DMA((9,))), 12, "prepare", 1 << 32, hbm=3)
    full = ((4, F, W), BF)
    join = lambda *v: local_call(join_kernel, v, (full,), (), 4, "join")[0]
    x2 = swap_chip(x0)
    xn = swap_core(join(mod, x0, x2))
    d_out, = local_call(relay_kernel, (x2, d0), (half,), (), 4, "relay")
    d2 = swap_chip(d_out)

    units, terms = ((144, W), BF), ((F, W), BF)
    u0, u1, u2, u3_low, u3_high, qk, soft, stat, back_w = local_call(
        latent_kernel, (turned, x0, x2, xn, mod, d_out, weights),
        (units,) * 3
        + (terms, ((80, W), BF), ((2 * F, W), BF), ((8 * F, F), F32), ((2 * F, 128), F32), ((4, W, W), BF)),
        (vmem((4, 2 * F, W), BF), vmem((2 * F, W), BF), vmem((144, W), BF), pltpu.SemaphoreType.DMA((4,))),
        16, "latents", 1 << 30, hbm=1)
    low, high = swap_core(u3_low), swap_core(u3_high)
    summed, = local_call(merge_kernel, (u2, low, high), (units,), (), 4, "merge")
    arrived = swap_chip(summed)
    dn = swap_core(join(summed, d0, d2))
    beside = swap_core(u1)

    v0, v2, v_send, ids_late = local_call(
        tangent_kernel,
        (x0, x2, xn, d0, d2, dn, u0, u1, u2, u3_low, u3_high, mod, stat, qk, soft, summed, weights, back_w),
        (terms, terms, ((2 * F, W), BF), ((F, 128), F32)),
        (vmem((4, 2 * F, W), BF), vmem((2 * F, W), BF), vmem((2 * F, W), BF), vmem((4, 2 * F, W), F32),
         vmem((4, F, W), BF)), 20, "tangent", 1 << 34)
    score, = local_call(
        score_kernel, (u0, beside, arrived, x0, mod, stat), (((F * 16, 128), BF),), (vmem((F * 16, 128), F32),), 6, "score")
    v_got = swap_core(v_send)
    v_sum, = local_call(add_kernel, (score, v2, v_got), (terms,), (), 4, "add")
    v_chip = swap_chip(v_sum)

    ready, = local_call(
        finish_kernel, (score, v0, v_got, v_chip), (((F * 24, 128), BF),), (vmem((F, 24, 128), F32),), 6, "finish")
    back = lax.all_to_all(ready, "seq", split_axis=0, concat_axis=0, tiled=True)
    score_field, table = local_call(
        tail_kernel, (back, ids_late), (((2 * F, W), BF), ((16, CONCEPTS), F32)),
        (vmem((F * 24, 128), F32), vmem((2 * F * 8, 128), F32)), 8, "tail")
    return (score_field.reshape(1, 2 * F, W), table.T)


def solution(mesh):
    in_specs = (
        P("seq", None, "tp"),
        P("seq", None, "tp"),
        P("seq"),
        P(),
        P(None, "tp"),
        P(None, "tp"),
        P(None, "tp"),
    )
    out_specs = (P("seq", None, "tp"), P(None, ("seq", "tp")))
    return jax.shard_map(body, mesh=mesh, in_specs=in_specs, out_specs=out_specs, check_vma=False)
```

```python
import math

import jax
import jax.numpy as jnp
from jax import lax
from jax.experimental import pallas as pl
from jax.experimental.pallas import tpu as pltpu
from jax.sharding import PartitionSpec as P

D = 4096
HD = 128
CONCEPTS = 256
STEPS = 1000
EPS = 1e-06
F = 64
W = 1024
STEP = 36

BF = jnp.bfloat16
F32 = jnp.float32
NT = (((1,), (1,)), ((), ()))


def nt(a, b):
    return lax.dot_general(a, b, NT, preferred_element_type=F32)


def turn_kernel(wq_ref, wk_ref, o_ref, token_ref, w_s, t_s, sems, out_sems):
    me = lax.axis_index("tp")
    copies, outs = [], []
    for k in range(4):
        rows = pl.ds(pl.multiple_of((me ^ k) * W, W), W)
        for i, ref in enumerate((wq_ref, wk_ref)):
            copy = pltpu.make_async_copy(ref.at[rows], w_s.at[k, :, pl.ds(512 * i, 512)], sems.at[2 * k + i])
            copy.start()
            copies.append(copy)
    for k in range(4):
        copies[2 * k].wait()
        copies[2 * k + 1].wait()
        for j in range(4):
            t_s[k, :, 256 * j:256 * j + 256] = w_s[k, 256 * j:256 * j + 256, :].T
        out = pltpu.make_async_copy(t_s.at[k], o_ref.at[k], out_sems.at[k])
        out.start()
        outs.append(out)
    for out in outs:
        out.wait()
    token_ref[...] = jnp.zeros_like(token_ref)


def prepare_kernel(wq_ref, wk_ref, turned_ref, table_ref, t1, t2, t3, ids_ref, steps_ref, w_ref, late_ref, mod_ref, t0, sems):
    me = lax.axis_index("tp")
    own = pltpu.make_async_copy(table_ref, t0, sems.at[8])
    own.start()
    copies = []
    for k in range(4):
        rows = pl.ds(pl.multiple_of((me ^ k) * W, W), W)
        for i, ref in enumerate((wq_ref, wk_ref)):
            copy = pltpu.make_async_copy(ref.at[rows], w_ref.at[k, :, pl.ds(512 * i, 512)], sems.at[2 * k + i])
            copy.start()
            copies.append(copy)
    for k in range(2):
        copy = pltpu.make_async_copy(turned_ref.at[2 + k], late_ref.at[k], sems.at[9 + k])
        copy.start()
        copies.append(copy)
    ids = ids_ref[:, 0:128].astype(F32)
    onehot = (ids[:, 0:1] == lax.broadcasted_iota(jnp.int32, (F, CONCEPTS), 1).astype(F32)).astype(BF)
    for k, ref in ((1, t1), (2, t2), (3, t3), (0, t0)):
        if k == 0:
            own.wait()
        mod_ref[k] = 1.0 + jnp.dot(onehot, ref[...], preferred_element_type=F32)
    mod_ref[4, :, 0:128] = ids
    mod_ref[4, :, 128:256] = jnp.zeros((F, 128), F32) + steps_ref[...]
    for copy in copies:
        copy.wait()


def relay_kernel(_, v_ref, o_ref):
    o_ref[...] = v_ref[...]


def join_kernel(_, a_ref, b_ref, o_ref):
    o_ref[0:2] = a_ref[...]
    o_ref[2:4] = b_ref[...]


def slices(own, chip, near):
    return [own.at[0:2], near.at[0:2], chip.at[0:2], near.at[2:4]]


def pack_kernel(x_ref, d_ref, concept_ref, o_ref, x_s, d_s, id_s, in_s, out_s, send_s, sems):
    y_hi = lax.axis_index("tp") >> 1
    copies = [
        pltpu.make_async_copy(src, dst, sems.at[i])
        for i, (src, dst) in enumerate(((x_ref, x_s), (d_ref, d_s), (concept_ref, id_s)))]
    for copy in copies:
        copy.start()
    for half, ref in enumerate((x_s, d_s)):
        copies[half].wait()
        for j in range(8):
            in_s[256 * j + 128 * half:256 * j + 128 * half + 128] = ref[:, 128 * j:128 * j + 128].astype(F32)
        for p in range(2):
            for j in range(8):
                rows = in_s[pl.ds(256 * j + 128 * half + p, F, stride=2), :]
                out_s[pl.ds(j * 4 + 2 * half + p, F, stride=STEP), :] = flip_rows(rows, y_hi)
    copies[2].wait()
    for q in range(4):
        out_s[pl.ds(32 + q, F, stride=STEP), :] = jnp.zeros((F, 128), F32) + id_s[0].astype(F32)
    outs = []
    for i in range(4):
        rows = pl.ds(16 * i, 16)
        send_s[rows] = out_s[16 * STEP * i:16 * STEP * i + 16 * STEP].astype(BF).reshape(16, 9, 4, 128)
        out = pltpu.make_async_copy(send_s.at[rows], o_ref.at[rows], sems.at[3 + i])
        out.start()
        outs.append(out)
    for out in outs:
        out.wait()


def flip_rows(v, y_hi):
    v = v.reshape(8, 8, 128)
    swapped = jnp.concatenate([v[:, 4:8], v[:, 0:4]], axis=1)
    return jnp.where(y_hi == 1, swapped, v).reshape(F, 128)


def unpack_kernel(_, g_ref, x_ref, d_ref, ids_ref, in_s):
    in_s[...] = g_ref[...].reshape(F * STEP, 128).astype(F32)
    for q in range(4):
        ref = (x_ref, d_ref)[q // 2]
        for j in range(8):
            ref[q % 2, :, 128 * j:128 * j + 128] = in_s[pl.ds(j * 4 + q, F, stride=STEP), :].astype(BF)
    ids_ref[:, 0:128] = in_s[pl.ds(32, F, stride=STEP), :].astype(BF)


def tail_kernel(g_ref, ids_ref, score_ref, table_ref, in_s, out_s):
    y_hi = lax.axis_index("tp") >> 1
    in_s[...] = g_ref[...].astype(F32)
    for p in range(2):
        for j in range(8):
            rows = in_s[pl.ds(p * 8 + j, F, stride=24), :]
            out_s[pl.ds(128 * j + p, F, stride=2), :] = flip_rows(rows, y_hi)
    for j in range(8):
        score_ref[:, 128 * j:128 * j + 128] = out_s[128 * j:128 * j + 128].astype(BF)
    total = jnp.sum(in_s[...].reshape(F, 24, 128)[:, 16:24], axis=0)
    cols = jnp.concatenate([total[:, 0:64], total[:, 64:128]], axis=0)
    ids = ids_ref[:, 0:1]
    onehot = (ids == lax.broadcasted_iota(jnp.int32, (F, CONCEPTS), 1).astype(F32)).astype(F32)
    table_ref[...] = jnp.dot(cols, onehot, precision=lax.Precision.HIGHEST, preferred_element_type=F32)


def forward(h_s, w_ref, out_ref):
    for part in range(4):
        cols = pl.ds(256 * part, 256)
        total = jnp.zeros((2 * F, 256), F32)
        for k in range(4):
            total = total + jnp.dot(h_s[k], w_ref[k, :, cols], preferred_element_type=F32)
        out_ref[:, cols] = total.astype(BF)


def eye128():
    return lax.broadcasted_iota(jnp.int32, (128, 128), 0) == lax.broadcasted_iota(jnp.int32, (128, 128), 1)


def spots():
    return [(pl.ds(64 * p, 64), pl.ds(128 * h, 128), pl.ds(512 + 128 * h, 128)) for p in range(2) for h in range(4)]


def latent_kernel(x0, x2, xn, mod_ref, _, w_ref, late_ref,
                  u2, u3_low, u3_high, qk_ref, soft_ref, stat_ref, g_s, h_s, u3):
    xs = slices(x0, x2, xn)
    sq = jnp.zeros((2 * F, 128), F32)
    for k in range(4):
        for j in range(8):
            x = xs[k][:, :, 128 * j:128 * j + 128].astype(F32).reshape(2 * F, 128)
            sq = sq + x * x
    inv = lax.rsqrt(jnp.sum(sq, axis=-1, keepdims=True) / D + EPS)
    lane = lax.broadcasted_iota(jnp.int32, (2 * F, 128), 1)
    stat_ref[...] = jnp.where(lane == 0, inv, 0.0)
    for k in range(4):
        for j in range(4):
            lanes = pl.ds(256 * j, 256)
            m = mod_ref[k, :, lanes]
            n = xs[k][:, :, lanes].astype(F32).reshape(2 * F, 256) * inv
            h_s[k, :, lanes] = (n * jnp.concatenate([m, m], axis=0)).astype(BF)
    forward(h_s, w_ref, qk_ref)

    temp = mod_ref[4, :, 128:192]
    where = spots()
    qs = [qk_ref[r, ql] for r, ql, _ in where]
    ks = [qk_ref[r, kl] for r, _, kl in where]
    scores = [nt(q, k) * temp for q, k in zip(qs, ks)]
    tops = [jnp.max(v, axis=-1, keepdims=True) for v in scores]
    exps = [jnp.exp(v - t) for v, t in zip(scores, tops)]
    sums = [jnp.sum(e, axis=-1, keepdims=True) for e in exps]
    ws = [e / v for e, v in zip(exps, sums)]
    for i, w in enumerate(ws):
        soft_ref[64 * i:64 * i + 64, :] = w
    gqs = [(-jnp.dot(w.astype(BF), k, preferred_element_type=F32)).astype(BF) for w, k in zip(ws, ks)]
    gks = [(-jnp.dot(w.T.astype(BF), q, preferred_element_type=F32)).astype(BF) for w, q in zip(ws, qs)]
    part = [jnp.zeros((F, HD), F32), jnp.zeros((F, HD), F32)]
    for i, (r, ql, kl) in enumerate(where):
        g_s[r, ql] = gqs[i]
        g_s[r, kl] = gks[i]
        part[i // 4] = part[i // 4] + gqs[i].astype(F32) * qs[i].astype(F32) + gks[i].astype(F32) * ks[i].astype(F32)
    scal = jnp.sum(jnp.concatenate(part, axis=0), axis=-1, keepdims=True)
    srow = jnp.sum(jnp.where(eye128(), scal, 0.0), axis=0, keepdims=True)
    hi = srow.astype(BF).astype(F32)
    sub = lax.broadcasted_iota(jnp.int32, (16, 128), 0)
    stats = jnp.where(sub == 0, hi, jnp.where(sub == 1, srow - hi, 0.0)).astype(BF)
    for ref, k in ((u3, 1), (u2, 0)):
        for j in range(4):
            lanes = pl.ds(256 * j, 256)
            ref[0:128, lanes] = jnp.dot(g_s[...], late_ref[k, :, lanes], preferred_element_type=F32).astype(BF)
        ref[128:144, 0:128] = stats
        ref[128:144, 128:1024] = jnp.zeros((16, 896), BF)
    u3_low[...] = u3[0:64, :]
    u3_high[...] = u3[64:144, :]


def normed_of(x_ref, d_ref, lanes, inv, mean):
    n = x_ref[:, :, lanes].astype(F32).reshape(2 * F, -1) * inv
    d = d_ref[:, :, lanes].astype(F32).reshape(2 * F, -1)
    return n, inv * (d - n * mean)


def tangent_kernel(x0, x2, xn, d0, d2, dn, u0, u1, u2, u3_low, u3_high, mod_ref, stat_ref, qk_ref, soft_ref,
                   w_ref, back_ref, late_ref, o0, o1, o2, o3, ids_ref, h_s, tan_s, g_s, drift_s, term_s):
    xs, ds = slices(x0, x2, xn), slices(d0, d2, dn)
    me = lax.axis_index("tp")
    ids_ref[...] = mod_ref[4, :, 0:128]
    sd = jnp.zeros((2 * F, 128), F32)
    for k in range(4):
        for j in range(8):
            x = xs[k][:, :, 128 * j:128 * j + 128].astype(F32).reshape(2 * F, 128)
            d = ds[k][:, :, 128 * j:128 * j + 128].astype(F32).reshape(2 * F, 128)
            sd = sd + x * d
    inv = jnp.sum(stat_ref[...], axis=-1, keepdims=True)
    mean = inv * (jnp.sum(sd, axis=-1, keepdims=True) / D)

    for k in range(4):
        for j in range(4):
            lanes = pl.ds(256 * j, 256)
            nd = normed_of(xs[k], ds[k], lanes, inv, mean)[1]
            m = mod_ref[k, :, lanes]
            h_s[k, :, lanes] = (nd * jnp.concatenate([m, m], axis=0)).astype(BF)
    forward(h_s, w_ref, tan_s)

    temp = mod_ref[4, :, 128:192]
    where = spots()
    qs = [qk_ref[r, ql] for r, ql, _ in where]
    ks = [qk_ref[r, kl] for r, _, kl in where]
    qts = [tan_s[r, ql] for r, ql, _ in where]
    kts = [tan_s[r, kl] for r, _, kl in where]
    ws = [soft_ref[64 * i:64 * i + 64, :] for i in range(8)]
    tdots = [nt(jnp.concatenate([a, b], axis=1), jnp.concatenate([c, d], axis=1)) for a, b, c, d in zip(qts, qs, ks, kts)]
    means = [jnp.sum(w * t, axis=-1, keepdims=True) for w, t in zip(ws, tdots)]
    curs = [temp * w * (t - m) for w, t, m in zip(ws, tdots, means)]
    cw = [jnp.concatenate([c, w], axis=1).astype(BF) for w, c in zip(ws, curs)]
    cwt = [jnp.concatenate([c, w], axis=0).T.astype(BF) for w, c in zip(ws, curs)]
    aqs = [jnp.dot(m, jnp.concatenate([k, kt], axis=0), preferred_element_type=F32) for m, k, kt in zip(cw, ks, kts)]
    aks = [jnp.dot(m, jnp.concatenate([q, qt], axis=0), preferred_element_type=F32) for m, q, qt in zip(cwt, qs, qts)]
    for i, (r, ql, kl) in enumerate(where):
        g_s[r, ql] = (-aqs[i]).astype(BF)
        g_s[r, kl] = (-aks[i]).astype(BF)

    for k in range(4):
        source = back_ref if k < 2 else late_ref
        for j in range(4):
            lanes = pl.ds(256 * j, 256)
            drift_s[k, :, lanes] = jnp.dot(g_s[...], source[k % 2, :, lanes], preferred_element_type=F32)

    rr = lax.broadcasted_iota(jnp.int32, (128, 256), 0)
    cc = lax.broadcasted_iota(jnp.int32, (128, 256), 1)
    pick = (((rr >> 3) & 3) == (cc >> 6)) & ((rr >> 5) == ((cc >> 4) & 3)) & ((rr & 7) == (cc & 7))
    pick = pick.astype(BF)
    late = ((lax.broadcasted_iota(jnp.int32, (F, 256), 1) >> 3) & 1) == 1
    for k in range(4):
        for j in range(4):
            lanes = pl.ds(256 * j, 256)
            n, nd = normed_of(xs[k], ds[k], lanes, inv, mean)
            if k == 3:
                units = jnp.concatenate([u3_low[:, lanes], u3_high[0:64, lanes]], axis=0)
            else:
                units = (u0, u1, u2)[k][0:128, lanes]
            terms = n * drift_s[k, :, lanes] + nd * units.astype(F32)
            terms = terms[0:64] + terms[64:128]
            split = jnp.concatenate([jnp.where(late, 0.0, terms), jnp.where(late, terms, 0.0)], axis=0).astype(BF)
            moved = nt(pick, split).astype(BF)
            spot = pl.ds(pl.multiple_of((me ^ k) * 256 + 128 * (j // 2), 128), 128)
            low = 32 * (j % 2)
            for t in range(4):
                term_s[t, low:low + 32, spot] = moved[32 * t:32 * t + 32]
    o0[...] = term_s[me]
    o2[...] = term_s[me ^ 2]
    o3[...] = term_s[me ^ 3]
    o1[...] = term_s[me ^ 1]


def local_call(kernel, args, outs, scratch, limit, name, flops=1 << 12, hbm=0):
    vm = pl.BlockSpec(memory_space=pltpu.VMEM)
    args = [pltpu.with_memory_space_constraint(v, pltpu.HBM) if i < hbm else v for i, v in enumerate(args)]
    return pl.pallas_call(
        kernel,
        out_shape=tuple(jax.ShapeDtypeStruct(s, t) for s, t in outs),
        in_specs=[pl.BlockSpec(memory_space=pltpu.HBM)] * hbm + [vm] * (len(args) - hbm),
        out_specs=tuple(vm for _ in outs),
        scratch_shapes=scratch,
        compiler_params=pltpu.CompilerParams(vmem_limit_bytes=limit * 1024 * 1024),
        cost_estimate=pl.CostEstimate(flops=flops, bytes_accessed=1 << 12, transcendentals=0),
        name=name,
    )(*args)


def add_kernel(_, a_ref, b_ref, o_ref):
    o_ref[...] = (a_ref[...].astype(F32) + b_ref[...].astype(F32)).astype(BF)


def merge_kernel(a_ref, low_ref, high_ref, first_ref, rest_ref):
    first_ref[...] = (a_ref[0:32, :].astype(F32) + low_ref[0:32, :].astype(F32)).astype(BF)
    rest_ref[0:32, :] = (a_ref[32:64, :].astype(F32) + low_ref[32:64, :].astype(F32)).astype(BF)
    rest_ref[32:96, :] = (a_ref[64:128, :].astype(F32) + high_ref[0:64, :].astype(F32)).astype(BF)
    rest_ref[96:112, :] = jnp.concatenate(
        [a_ref[128:144, 0:128], high_ref[64:80, 0:128], a_ref[128:144, 256:1024]], axis=1)


def others_kernel(turned_ref, _, grad_ref, u2, back_ref, u0, u1, sems):
    copies = [pltpu.make_async_copy(turned_ref.at[k], back_ref.at[k], sems.at[k]) for k in range(2)]
    for copy in copies:
        copy.start()
    for k, ref in enumerate((u0, u1)):
        copies[k].wait()
        for j in range(4):
            lanes = pl.ds(256 * j, 256)
            ref[0:128, lanes] = jnp.dot(grad_ref[...], back_ref[k, :, lanes], preferred_element_type=F32).astype(BF)
        ref[128:144, :] = u2[128:144, :]


def score_kernel(a_ref, b_ref, first_ref, rest_ref, x_ref, mod_ref, stat_ref, score_ref, out_s):
    srow = jnp.zeros((1, 128), F32)
    for ref, row, lane in ((a_ref, 128, 0), (b_ref, 128, 0), (rest_ref, 96, 0), (rest_ref, 96, 128)):
        part = ref[row:row + 16, lane:lane + 128].astype(F32)
        srow = srow + (part[0:1] + part[1:2])
    mean = jnp.sum(jnp.where(eye128(), srow, 0.0), axis=1, keepdims=True) / D
    inv = jnp.sum(stat_ref[...], axis=1, keepdims=True)
    for j in range(4):
        lanes = pl.ds(256 * j, 256)
        far = jnp.concatenate([first_ref[:, lanes], rest_ref[0:96, lanes]], axis=0).astype(F32)
        units = (a_ref[0:128, lanes].astype(F32) + b_ref[0:128, lanes].astype(F32)) + far
        mod = mod_ref[0, :, lanes]
        mod = jnp.concatenate([mod, mod], axis=0)
        x = x_ref[:, :, lanes].astype(F32).reshape(2 * F, 256)
        score = inv * (mod * units - (x * inv) * mean)
        for p in range(2):
            for i in range(2):
                out_s[pl.ds(8 * p + 2 * j + i, F, stride=16), :] = score[64 * p:64 * p + 64, 128 * i:128 * i + 128]
    score_ref[...] = out_s[...].astype(BF)


def finish_kernel(score_ref, a_ref, b_ref, c_ref, o_ref, out_s):
    out_s[:, 0:16] = score_ref[...].astype(F32).reshape(F, 16, 128)
    total = (a_ref[...].astype(F32) + b_ref[...].astype(F32)) + c_ref[...].astype(F32)
    for j in range(8):
        out_s[8 * j:8 * j + 8, 16:24] = total[:, 128 * j:128 * j + 128].reshape(8, 8, 128)
    o_ref[...] = out_s[...].reshape(F * 24, 128).astype(BF)


def body(latent, direction, concept, timestep, concept_table, w_query, w_key):
    cross = []
    for s in range(64):
        for t in range(4):
            cross.append((4 * s + t, 4 * (s ^ 4) + (t ^ 2)))
    core = [(t, t ^ 1) for t in range(4)]
    swap_core = lambda v: lax.ppermute(v, "tp", core)
    swap_chip = lambda v: lax.ppermute(v, ("seq", "tp"), cross)
    vmem = pltpu.VMEM

    hbm = pl.BlockSpec(memory_space=pltpu.HBM)
    sent = pl.pallas_call(
        pack_kernel,
        out_shape=jax.ShapeDtypeStruct((F, 9, 4, 128), BF),
        in_specs=[hbm, hbm, pl.BlockSpec(memory_space=pl.ANY)],
        out_specs=hbm,
        scratch_shapes=[
            vmem((2 * F, W), BF), vmem((2 * F, W), BF), pltpu.SMEM((1,), jnp.int32), vmem((4 * F * 8, 128), F32),
            vmem((F * STEP, 128), F32), vmem((F, 9, 4, 128), BF), pltpu.SemaphoreType.DMA((7,))],
        compiler_params=pltpu.CompilerParams(vmem_limit_bytes=8 * 1024 * 1024),
        name="pack",
    )(*[pltpu.with_memory_space_constraint(v.reshape(2 * F, W), pltpu.HBM) for v in (latent, direction)], concept)
    got = lax.all_to_all(sent, "seq", split_axis=0, concat_axis=0, tiled=True)

    turned, token = pl.pallas_call(
        turn_kernel,
        out_shape=(jax.ShapeDtypeStruct((4, W, W), BF), jax.ShapeDtypeStruct((8, 128), F32)),
        in_specs=[hbm, hbm],
        out_specs=(hbm, pl.BlockSpec(memory_space=pltpu.VMEM)),
        scratch_shapes=[vmem((4, W, W), BF), vmem((4, W, W), BF),
                        pltpu.SemaphoreType.DMA((8,)), pltpu.SemaphoreType.DMA((4,))],
        compiler_params=pltpu.CompilerParams(vmem_limit_bytes=24 * 1024 * 1024),
        cost_estimate=pl.CostEstimate(flops=1 << 33, bytes_accessed=1 << 24, transcendentals=0),
        name="turn",
    )(pltpu.with_memory_space_constraint(w_query, pltpu.HBM), pltpu.with_memory_space_constraint(w_key, pltpu.HBM))
    t_core = swap_core(concept_table)
    t_chip = swap_chip(concept_table)
    t_both = swap_core(t_chip)

    half = ((2, F, W), BF)
    x0, d0, ids = local_call(
        unpack_kernel, (token, got), (half, half, ((F, 2 * W), BF)), (vmem((F * STEP, 128), F32),), 8, "unpack")

    steps = ((0.25 + 1.75 * timestep.astype(F32) / STEPS) / math.sqrt(HD)).reshape(F, 1)
    weights, back_late, mod = local_call(
        prepare_kernel, (w_query, w_key, turned, concept_table, t_core, t_chip, t_both, ids, steps),
        (((4, W, W), BF), ((2, W, W), BF), ((5, F, W), F32)),
        (vmem((CONCEPTS, W), BF), pltpu.SemaphoreType.DMA((11,))), 16, "prepare", 1 << 32, hbm=4)
    full = ((4, F, W), BF)
    join = lambda *v: local_call(join_kernel, v, (full,), (), 4, "join")[0]
    x2 = swap_chip(x0)
    xn = swap_core(join(mod, x0, x2))
    d_out, = local_call(relay_kernel, (x2, d0), (half,), (), 4, "relay")
    d2 = swap_chip(d_out)

    units, terms = ((144, W), BF), ((F, W), BF)
    u2, u3_low, u3_high, qk, soft, stat, grads = local_call(
        latent_kernel, (x0, x2, xn, mod, d_out, weights, back_late),
        (units, terms, ((80, W), BF), ((2 * F, W), BF), ((8 * F, F), F32), ((2 * F, 128), F32), ((2 * F, W), BF)),
        (vmem((4, 2 * F, W), BF), vmem((144, W), BF)), 16, "latents", 1 << 30)
    low, high = swap_core(u3_low), swap_core(u3_high)
    first, rest = local_call(
        merge_kernel, (u2, low, high), (((32, W), BF), ((112, W), BF)), (), 4, "merge")
    back_w, u0, u1 = local_call(
        others_kernel, (turned, first, grads, u2), (((2, W, W), BF), units, units), (pltpu.SemaphoreType.DMA((2,)),),
        8, "others", 1 << 12, hbm=1)
    dn = swap_core(join(u0, d0, d2))
    got_first = swap_chip(first)
    rest, = local_call(relay_kernel, (got_first, rest), (((112, W), BF),), (), 4, "relay", 1 << 34)
    got_rest = swap_chip(rest)
    v0, v1, v2, v3, ids_late = local_call(
        tangent_kernel,
        (x0, x2, xn, d0, d2, dn, u0, u1, u2, u3_low, u3_high, mod, stat, qk, soft, weights, back_w, back_late),
        (terms,) * 4 + (((F, 128), F32),),
        (vmem((4, 2 * F, W), BF), vmem((2 * F, W), BF), vmem((2 * F, W), BF), vmem((4, 2 * F, W), F32),
         vmem((4, F, W), BF)), 20, "tangent", 1 << 34)
    beside = swap_core(u1)
    score, = local_call(
        score_kernel, (u0, beside, got_first, got_rest, x0, mod, stat), (((F * 16, 128), BF),), (vmem((F * 16, 128), F32),), 6, "score")
    v_far, v_near = swap_core(v3), swap_core(v1)
    v_sum, = local_call(add_kernel, (got_rest, v2, v_far), (terms,), (), 4, "add")
    v_chip = swap_chip(v_sum)

    ready, = local_call(
        finish_kernel, (score, v0, v_near, v_chip), (((F * 24, 128), BF),), (vmem((F, 24, 128), F32),), 6, "finish")
    back = lax.all_to_all(ready, "seq", split_axis=0, concat_axis=0, tiled=True)
    score_field, table = local_call(
        tail_kernel, (back, ids_late), (((2 * F, W), BF), ((16, CONCEPTS), F32)),
        (vmem((F * 24, 128), F32), vmem((2 * F * 8, 128), F32)), 8, "tail")
    return (score_field.reshape(1, 2 * F, W), table.T)


def solution(mesh):
    in_specs = (
        P("seq", None, "tp"),
        P("seq", None, "tp"),
        P("seq"),
        P(),
        P(None, "tp"),
        P(None, "tp"),
        P(None, "tp"),
    )
    out_specs = (P("seq", None, "tp"), P(None, ("seq", "tp")))
    return jax.shard_map(body, mesh=mesh, in_specs=in_specs, out_specs=out_specs, check_vma=False)
```

```python
import math

import jax
import jax.numpy as jnp
from jax import lax
from jax.experimental import pallas as pl
from jax.experimental.pallas import tpu as pltpu
from jax.sharding import PartitionSpec as P

D = 4096
HD = 128
CONCEPTS = 256
STEPS = 1000
EPS = 1e-06
F = 64
W = 1024
STEP = 36

BF = jnp.bfloat16
F32 = jnp.float32
NT = (((1,), (1,)), ((), ()))


def nt(a, b):
    return lax.dot_general(a, b, NT, preferred_element_type=F32)


def turn_kernel(wq_ref, wk_ref, o_ref, token_ref, w_s, t_s, sems, out_sems):
    me = lax.axis_index("tp")
    copies, outs = [], []
    for k in range(4):
        rows = pl.ds(pl.multiple_of((me ^ k) * W, W), W)
        for i, ref in enumerate((wq_ref, wk_ref)):
            copy = pltpu.make_async_copy(ref.at[rows], w_s.at[k, :, pl.ds(512 * i, 512)], sems.at[2 * k + i])
            copy.start()
            copies.append(copy)
    for k in range(4):
        copies[2 * k].wait()
        copies[2 * k + 1].wait()
        for j in range(4):
            t_s[k, :, 256 * j:256 * j + 256] = w_s[k, 256 * j:256 * j + 256, :].T
        out = pltpu.make_async_copy(t_s.at[k], o_ref.at[k], out_sems.at[k])
        out.start()
        outs.append(out)
    for out in outs:
        out.wait()
    token_ref[...] = jnp.zeros_like(token_ref)


def prepare_kernel(wq_ref, wk_ref, turned_ref, table_ref, t1, t2, t3, ids_ref, steps_ref, w_ref, late_ref, mod_ref, t0, sems):
    me = lax.axis_index("tp")
    own = pltpu.make_async_copy(table_ref, t0, sems.at[8])
    own.start()
    copies = []
    for k in range(4):
        rows = pl.ds(pl.multiple_of((me ^ k) * W, W), W)
        for i, ref in enumerate((wq_ref, wk_ref)):
            copy = pltpu.make_async_copy(ref.at[rows], w_ref.at[k, :, pl.ds(512 * i, 512)], sems.at[2 * k + i])
            copy.start()
            copies.append(copy)
    for k in range(3):
        copy = pltpu.make_async_copy(turned_ref.at[1 + k], late_ref.at[k], sems.at[9 + k])
        copy.start()
        copies.append(copy)
    ids = ids_ref[:, 0:128].astype(F32)
    onehot = (ids[:, 0:1] == lax.broadcasted_iota(jnp.int32, (F, CONCEPTS), 1).astype(F32)).astype(BF)
    for k, ref in ((1, t1), (2, t2), (3, t3), (0, t0)):
        if k == 0:
            own.wait()
        mod_ref[k] = 1.0 + jnp.dot(onehot, ref[...], preferred_element_type=F32)
    mod_ref[4, :, 0:128] = ids
    mod_ref[4, :, 128:256] = jnp.zeros((F, 128), F32) + steps_ref[...]
    for copy in copies:
        copy.wait()


def relay_kernel(_, v_ref, o_ref):
    o_ref[...] = v_ref[...]


def join_kernel(_, a_ref, b_ref, o_ref):
    o_ref[0:2] = a_ref[...]
    o_ref[2:4] = b_ref[...]


def slices(own, chip, near):
    return [own.at[0:2], near.at[0:2], chip.at[0:2], near.at[2:4]]


def pack_kernel(x_ref, d_ref, concept_ref, o_ref, x_s, d_s, id_s, in_s, out_s, send_s, sems):
    y_hi = lax.axis_index("tp") >> 1
    copies = [
        pltpu.make_async_copy(src, dst, sems.at[i])
        for i, (src, dst) in enumerate(((x_ref, x_s), (d_ref, d_s), (concept_ref, id_s)))]
    for copy in copies:
        copy.start()
    for half, ref in enumerate((x_s, d_s)):
        copies[half].wait()
        for j in range(8):
            in_s[256 * j + 128 * half:256 * j + 128 * half + 128] = ref[:, 128 * j:128 * j + 128].astype(F32)
        for p in range(2):
            for j in range(8):
                rows = in_s[pl.ds(256 * j + 128 * half + p, F, stride=2), :]
                out_s[pl.ds(j * 4 + 2 * half + p, F, stride=STEP), :] = flip_rows(rows, y_hi)
    copies[2].wait()
    for q in range(4):
        out_s[pl.ds(32 + q, F, stride=STEP), :] = jnp.zeros((F, 128), F32) + id_s[0].astype(F32)
    outs = []
    for i in range(4):
        rows = pl.ds(16 * i, 16)
        send_s[rows] = out_s[16 * STEP * i:16 * STEP * i + 16 * STEP].astype(BF).reshape(16, 9, 4, 128)
        out = pltpu.make_async_copy(send_s.at[rows], o_ref.at[rows], sems.at[3 + i])
        out.start()
        outs.append(out)
    for out in outs:
        out.wait()


def flip_rows(v, y_hi):
    v = v.reshape(8, 8, 128)
    swapped = jnp.concatenate([v[:, 4:8], v[:, 0:4]], axis=1)
    return jnp.where(y_hi == 1, swapped, v).reshape(F, 128)


def unpack_kernel(_, g_ref, x_ref, d_ref, ids_ref, in_s):
    in_s[...] = g_ref[...].reshape(F * STEP, 128).astype(F32)
    for q in range(4):
        ref = (x_ref, d_ref)[q // 2]
        for j in range(8):
            ref[q % 2, :, 128 * j:128 * j + 128] = in_s[pl.ds(j * 4 + q, F, stride=STEP), :].astype(BF)
    ids_ref[:, 0:128] = in_s[pl.ds(32, F, stride=STEP), :].astype(BF)


def tail_kernel(g_ref, ids_ref, score_ref, table_ref, in_s, out_s):
    y_hi = lax.axis_index("tp") >> 1
    in_s[...] = g_ref[...].astype(F32)
    for p in range(2):
        for j in range(8):
            rows = in_s[pl.ds(p * 8 + j, F, stride=24), :]
            out_s[pl.ds(128 * j + p, F, stride=2), :] = flip_rows(rows, y_hi)
    for j in range(8):
        score_ref[:, 128 * j:128 * j + 128] = out_s[128 * j:128 * j + 128].astype(BF)
    total = jnp.sum(in_s[...].reshape(F, 24, 128)[:, 16:24], axis=0)
    cols = jnp.concatenate([total[:, 0:64], total[:, 64:128]], axis=0)
    ids = ids_ref[:, 0:1]
    onehot = (ids == lax.broadcasted_iota(jnp.int32, (F, CONCEPTS), 1).astype(F32)).astype(F32)
    table_ref[...] = jnp.dot(cols, onehot, precision=lax.Precision.HIGHEST, preferred_element_type=F32)


def forward(h_s, w_ref, out_ref):
    for part in range(4):
        cols = pl.ds(256 * part, 256)
        total = jnp.zeros((2 * F, 256), F32)
        for k in range(4):
            total = total + jnp.dot(h_s[k], w_ref[k, :, cols], preferred_element_type=F32)
        out_ref[:, cols] = total.astype(BF)


def eye128():
    return lax.broadcasted_iota(jnp.int32, (128, 128), 0) == lax.broadcasted_iota(jnp.int32, (128, 128), 1)


def spots():
    return [(pl.ds(64 * p, 64), pl.ds(128 * h, 128), pl.ds(512 + 128 * h, 128)) for p in range(2) for h in range(4)]


def latent_kernel(x0, x2, xn, mod_ref, _, w_ref, late_ref,
                  u2, u3_low, u3_high, qk_ref, soft_ref, stat_ref, g_s, h_s, u3):
    xs = slices(x0, x2, xn)
    sq = jnp.zeros((2 * F, 128), F32)
    for k in range(4):
        for j in range(8):
            x = xs[k][:, :, 128 * j:128 * j + 128].astype(F32).reshape(2 * F, 128)
            sq = sq + x * x
    inv = lax.rsqrt(jnp.sum(sq, axis=-1, keepdims=True) / D + EPS)
    lane = lax.broadcasted_iota(jnp.int32, (2 * F, 128), 1)
    stat_ref[...] = jnp.where(lane == 0, inv, 0.0)
    for k in range(4):
        for j in range(4):
            lanes = pl.ds(256 * j, 256)
            m = mod_ref[k, :, lanes]
            n = xs[k][:, :, lanes].astype(F32).reshape(2 * F, 256) * inv
            h_s[k, :, lanes] = (n * jnp.concatenate([m, m], axis=0)).astype(BF)
    forward(h_s, w_ref, qk_ref)

    temp = mod_ref[4, :, 128:192]
    where = spots()
    qs = [qk_ref[r, ql] for r, ql, _ in where]
    ks = [qk_ref[r, kl] for r, _, kl in where]
    scores = [nt(q, k) * temp for q, k in zip(qs, ks)]
    tops = [jnp.max(v, axis=-1, keepdims=True) for v in scores]
    exps = [jnp.exp(v - t) for v, t in zip(scores, tops)]
    sums = [jnp.sum(e, axis=-1, keepdims=True) for e in exps]
    ws = [e / v for e, v in zip(exps, sums)]
    for i, w in enumerate(ws):
        soft_ref[64 * i:64 * i + 64, :] = w
    gqs = [(-jnp.dot(w.astype(BF), k, preferred_element_type=F32)).astype(BF) for w, k in zip(ws, ks)]
    gks = [(-jnp.dot(w.T.astype(BF), q, preferred_element_type=F32)).astype(BF) for w, q in zip(ws, qs)]
    part = [jnp.zeros((F, HD), F32), jnp.zeros((F, HD), F32)]
    for i, (r, ql, kl) in enumerate(where):
        g_s[r, ql] = gqs[i]
        g_s[r, kl] = gks[i]
        part[i // 4] = part[i // 4] + gqs[i].astype(F32) * qs[i].astype(F32) + gks[i].astype(F32) * ks[i].astype(F32)
    scal = jnp.sum(jnp.concatenate(part, axis=0), axis=-1, keepdims=True)
    srow = jnp.sum(jnp.where(eye128(), scal, 0.0), axis=0, keepdims=True)
    hi = srow.astype(BF).astype(F32)
    sub = lax.broadcasted_iota(jnp.int32, (16, 128), 0)
    stats = jnp.where(sub == 0, hi, jnp.where(sub == 1, srow - hi, 0.0)).astype(BF)
    for ref, k in ((u3, 2), (u2, 1)):
        for j in range(4):
            lanes = pl.ds(256 * j, 256)
            ref[0:128, lanes] = jnp.dot(g_s[...], late_ref[k, :, lanes], preferred_element_type=F32).astype(BF)
        ref[128:144, 0:128] = stats
        ref[128:144, 128:1024] = jnp.zeros((16, 896), BF)
    u3_low[...] = u3[0:64, :]
    u3_high[...] = u3[64:144, :]


def normed_of(x_ref, d_ref, lanes, inv, mean):
    n = x_ref[:, :, lanes].astype(F32).reshape(2 * F, -1) * inv
    d = d_ref[:, :, lanes].astype(F32).reshape(2 * F, -1)
    return n, inv * (d - n * mean)


def tangent_kernel(x0, x2, xn, d0, d2, dn, u0, u1, u2, u3_low, u3_high, mod_ref, stat_ref, qk_ref, soft_ref,
                   w_ref, back_ref, late_ref, o0, o1, o2, o3, ids_ref, h_s, tan_s, g_s, drift_s, term_s):
    xs, ds = slices(x0, x2, xn), slices(d0, d2, dn)
    me = lax.axis_index("tp")
    ids_ref[...] = mod_ref[4, :, 0:128]
    sd = jnp.zeros((2 * F, 128), F32)
    for k in range(4):
        for j in range(8):
            x = xs[k][:, :, 128 * j:128 * j + 128].astype(F32).reshape(2 * F, 128)
            d = ds[k][:, :, 128 * j:128 * j + 128].astype(F32).reshape(2 * F, 128)
            sd = sd + x * d
    inv = jnp.sum(stat_ref[...], axis=-1, keepdims=True)
    mean = inv * (jnp.sum(sd, axis=-1, keepdims=True) / D)

    for k in range(4):
        for j in range(4):
            lanes = pl.ds(256 * j, 256)
            nd = normed_of(xs[k], ds[k], lanes, inv, mean)[1]
            m = mod_ref[k, :, lanes]
            h_s[k, :, lanes] = (nd * jnp.concatenate([m, m], axis=0)).astype(BF)
    forward(h_s, w_ref, tan_s)

    temp = mod_ref[4, :, 128:192]
    where = spots()
    qs = [qk_ref[r, ql] for r, ql, _ in where]
    ks = [qk_ref[r, kl] for r, _, kl in where]
    qts = [tan_s[r, ql] for r, ql, _ in where]
    kts = [tan_s[r, kl] for r, _, kl in where]
    ws = [soft_ref[64 * i:64 * i + 64, :] for i in range(8)]
    tdots = [nt(jnp.concatenate([a, b], axis=1), jnp.concatenate([c, d], axis=1)) for a, b, c, d in zip(qts, qs, ks, kts)]
    means = [jnp.sum(w * t, axis=-1, keepdims=True) for w, t in zip(ws, tdots)]
    curs = [temp * w * (t - m) for w, t, m in zip(ws, tdots, means)]
    cw = [jnp.concatenate([c, w], axis=1).astype(BF) for w, c in zip(ws, curs)]
    cwt = [jnp.concatenate([c, w], axis=0).T.astype(BF) for w, c in zip(ws, curs)]
    aqs = [jnp.dot(m, jnp.concatenate([k, kt], axis=0), preferred_element_type=F32) for m, k, kt in zip(cw, ks, kts)]
    aks = [jnp.dot(m, jnp.concatenate([q, qt], axis=0), preferred_element_type=F32) for m, q, qt in zip(cwt, qs, qts)]
    for i, (r, ql, kl) in enumerate(where):
        g_s[r, ql] = (-aqs[i]).astype(BF)
        g_s[r, kl] = (-aks[i]).astype(BF)

    for k in range(4):
        for j in range(4):
            lanes = pl.ds(256 * j, 256)
            block = back_ref[:, lanes] if k == 0 else late_ref[k - 1, :, lanes]
            drift_s[k, :, lanes] = jnp.dot(g_s[...], block, preferred_element_type=F32)

    rr = lax.broadcasted_iota(jnp.int32, (128, 256), 0)
    cc = lax.broadcasted_iota(jnp.int32, (128, 256), 1)
    pick = (((rr >> 3) & 3) == (cc >> 6)) & ((rr >> 5) == ((cc >> 4) & 3)) & ((rr & 7) == (cc & 7))
    pick = pick.astype(BF)
    late = ((lax.broadcasted_iota(jnp.int32, (F, 256), 1) >> 3) & 1) == 1
    for k in range(4):
        for j in range(4):
            lanes = pl.ds(256 * j, 256)
            n, nd = normed_of(xs[k], ds[k], lanes, inv, mean)
            if k == 3:
                units = jnp.concatenate([u3_low[:, lanes], u3_high[0:64, lanes]], axis=0)
            else:
                units = (u0, u1, u2)[k][0:128, lanes]
            terms = n * drift_s[k, :, lanes] + nd * units.astype(F32)
            terms = terms[0:64] + terms[64:128]
            split = jnp.concatenate([jnp.where(late, 0.0, terms), jnp.where(late, terms, 0.0)], axis=0).astype(BF)
            moved = nt(pick, split).astype(BF)
            spot = pl.ds(pl.multiple_of((me ^ k) * 256 + 128 * (j // 2), 128), 128)
            low = 32 * (j % 2)
            for t in range(4):
                term_s[t, low:low + 32, spot] = moved[32 * t:32 * t + 32]
    o0[...] = term_s[me]
    o2[...] = term_s[me ^ 2]
    o3[...] = term_s[me ^ 3]
    o1[...] = term_s[me ^ 1]


def local_call(kernel, args, outs, scratch, limit, name, flops=1 << 12, hbm=0):
    vm = pl.BlockSpec(memory_space=pltpu.VMEM)
    args = [pltpu.with_memory_space_constraint(v, pltpu.HBM) if i < hbm else v for i, v in enumerate(args)]
    return pl.pallas_call(
        kernel,
        out_shape=tuple(jax.ShapeDtypeStruct(s, t) for s, t in outs),
        in_specs=[pl.BlockSpec(memory_space=pltpu.HBM)] * hbm + [vm] * (len(args) - hbm),
        out_specs=tuple(vm for _ in outs),
        scratch_shapes=scratch,
        compiler_params=pltpu.CompilerParams(vmem_limit_bytes=limit * 1024 * 1024),
        cost_estimate=pl.CostEstimate(flops=flops, bytes_accessed=1 << 12, transcendentals=0),
        name=name,
    )(*args)


def add_kernel(_, a_ref, b_ref, o_ref):
    o_ref[...] = (a_ref[...].astype(F32) + b_ref[...].astype(F32)).astype(BF)


def merge_kernel(a_ref, low_ref, high_ref, first_ref, rest_ref):
    first_ref[...] = (a_ref[0:32, :].astype(F32) + low_ref[0:32, :].astype(F32)).astype(BF)
    rest_ref[0:32, :] = (a_ref[32:64, :].astype(F32) + low_ref[32:64, :].astype(F32)).astype(BF)
    rest_ref[32:96, :] = (a_ref[64:128, :].astype(F32) + high_ref[0:64, :].astype(F32)).astype(BF)
    rest_ref[96:112, :] = jnp.concatenate(
        [a_ref[128:144, 0:128], high_ref[64:80, 0:128], a_ref[128:144, 256:1024]], axis=1)


def others_kernel(turned_ref, _, grad_ref, u2, late_ref, back_ref, u0, u1, sem):
    copy = pltpu.make_async_copy(turned_ref.at[0], back_ref, sem)
    copy.start()
    for k, ref in ((1, u1), (0, u0)):
        if k == 0:
            copy.wait()
        for j in range(4):
            lanes = pl.ds(256 * j, 256)
            block = back_ref[:, lanes] if k == 0 else late_ref[0, :, lanes]
            ref[0:128, lanes] = jnp.dot(grad_ref[...], block, preferred_element_type=F32).astype(BF)
        ref[128:144, :] = u2[128:144, :]


def score_kernel(a_ref, b_ref, first_ref, rest_ref, x_ref, mod_ref, stat_ref, score_ref, out_s):
    srow = jnp.zeros((1, 128), F32)
    for ref, row, lane in ((a_ref, 128, 0), (b_ref, 128, 0), (rest_ref, 96, 0), (rest_ref, 96, 128)):
        part = ref[row:row + 16, lane:lane + 128].astype(F32)
        srow = srow + (part[0:1] + part[1:2])
    mean = jnp.sum(jnp.where(eye128(), srow, 0.0), axis=1, keepdims=True) / D
    inv = jnp.sum(stat_ref[...], axis=1, keepdims=True)
    for j in range(4):
        lanes = pl.ds(256 * j, 256)
        far = jnp.concatenate([first_ref[:, lanes], rest_ref[0:96, lanes]], axis=0).astype(F32)
        units = (a_ref[0:128, lanes].astype(F32) + b_ref[0:128, lanes].astype(F32)) + far
        mod = mod_ref[0, :, lanes]
        mod = jnp.concatenate([mod, mod], axis=0)
        x = x_ref[:, :, lanes].astype(F32).reshape(2 * F, 256)
        score = inv * (mod * units - (x * inv) * mean)
        for p in range(2):
            for i in range(2):
                out_s[pl.ds(8 * p + 2 * j + i, F, stride=16), :] = score[64 * p:64 * p + 64, 128 * i:128 * i + 128]
    score_ref[...] = out_s[...].astype(BF)


def finish_kernel(score_ref, a_ref, b_ref, c_ref, o_ref, out_s):
    out_s[:, 0:16] = score_ref[...].astype(F32).reshape(F, 16, 128)
    total = (a_ref[...].astype(F32) + b_ref[...].astype(F32)) + c_ref[...].astype(F32)
    for j in range(8):
        out_s[8 * j:8 * j + 8, 16:24] = total[:, 128 * j:128 * j + 128].reshape(8, 8, 128)
    o_ref[...] = out_s[...].reshape(F * 24, 128).astype(BF)


def body(latent, direction, concept, timestep, concept_table, w_query, w_key):
    cross = []
    for s in range(64):
        for t in range(4):
            cross.append((4 * s + t, 4 * (s ^ 4) + (t ^ 2)))
    core = [(t, t ^ 1) for t in range(4)]
    swap_core = lambda v: lax.ppermute(v, "tp", core)
    swap_chip = lambda v: lax.ppermute(v, ("seq", "tp"), cross)
    vmem = pltpu.VMEM

    hbm = pl.BlockSpec(memory_space=pltpu.HBM)
    sent = pl.pallas_call(
        pack_kernel,
        out_shape=jax.ShapeDtypeStruct((F, 9, 4, 128), BF),
        in_specs=[hbm, hbm, pl.BlockSpec(memory_space=pl.ANY)],
        out_specs=hbm,
        scratch_shapes=[
            vmem((2 * F, W), BF), vmem((2 * F, W), BF), pltpu.SMEM((1,), jnp.int32), vmem((4 * F * 8, 128), F32),
            vmem((F * STEP, 128), F32), vmem((F, 9, 4, 128), BF), pltpu.SemaphoreType.DMA((7,))],
        compiler_params=pltpu.CompilerParams(vmem_limit_bytes=8 * 1024 * 1024),
        name="pack",
    )(*[pltpu.with_memory_space_constraint(v.reshape(2 * F, W), pltpu.HBM) for v in (latent, direction)], concept)
    got = lax.all_to_all(sent, "seq", split_axis=0, concat_axis=0, tiled=True)

    turned, token = pl.pallas_call(
        turn_kernel,
        out_shape=(jax.ShapeDtypeStruct((4, W, W), BF), jax.ShapeDtypeStruct((8, 128), F32)),
        in_specs=[hbm, hbm],
        out_specs=(hbm, pl.BlockSpec(memory_space=pltpu.VMEM)),
        scratch_shapes=[vmem((4, W, W), BF), vmem((4, W, W), BF),
                        pltpu.SemaphoreType.DMA((8,)), pltpu.SemaphoreType.DMA((4,))],
        compiler_params=pltpu.CompilerParams(vmem_limit_bytes=24 * 1024 * 1024),
        cost_estimate=pl.CostEstimate(flops=1 << 33, bytes_accessed=1 << 24, transcendentals=0),
        name="turn",
    )(pltpu.with_memory_space_constraint(w_query, pltpu.HBM), pltpu.with_memory_space_constraint(w_key, pltpu.HBM))
    t_core = swap_core(concept_table)
    t_chip = swap_chip(concept_table)
    t_both = swap_core(t_chip)

    half = ((2, F, W), BF)
    x0, d0, ids = local_call(
        unpack_kernel, (token, got), (half, half, ((F, 2 * W), BF)), (vmem((F * STEP, 128), F32),), 8, "unpack")

    steps = ((0.25 + 1.75 * timestep.astype(F32) / STEPS) / math.sqrt(HD)).reshape(F, 1)
    weights, back_late, mod = local_call(
        prepare_kernel, (w_query, w_key, turned, concept_table, t_core, t_chip, t_both, ids, steps),
        (((4, W, W), BF), ((3, W, W), BF), ((5, F, W), F32)),
        (vmem((CONCEPTS, W), BF), pltpu.SemaphoreType.DMA((12,))), 18, "prepare", 1 << 32, hbm=4)
    full = ((4, F, W), BF)
    join = lambda *v: local_call(join_kernel, v, (full,), (), 4, "join")[0]
    x2 = swap_chip(x0)
    xn = swap_core(join(mod, x0, x2))
    d_out, = local_call(relay_kernel, (x2, d0), (half,), (), 4, "relay")
    d2 = swap_chip(d_out)

    units, terms = ((144, W), BF), ((F, W), BF)
    u2, u3_low, u3_high, qk, soft, stat, grads = local_call(
        latent_kernel, (x0, x2, xn, mod, d_out, weights, back_late),
        (units, terms, ((80, W), BF), ((2 * F, W), BF), ((8 * F, F), F32), ((2 * F, 128), F32), ((2 * F, W), BF)),
        (vmem((4, 2 * F, W), BF), vmem((144, W), BF)), 16, "latents", 1 << 30)
    low, high = swap_core(u3_low), swap_core(u3_high)
    first, rest = local_call(
        merge_kernel, (u2, low, high), (((32, W), BF), ((112, W), BF)), (), 4, "merge")
    back_w, u0, u1 = local_call(
        others_kernel, (turned, first, grads, u2, back_late), (((W, W), BF), units, units), (pltpu.SemaphoreType.DMA,),
        8, "others", 1 << 12, hbm=1)
    dn = swap_core(join(u0, d0, d2))
    got_first = swap_chip(first)
    rest, = local_call(relay_kernel, (got_first, rest), (((112, W), BF),), (), 4, "relay", 1 << 34)
    got_rest = swap_chip(rest)
    v0, v1, v2, v3, ids_late = local_call(
        tangent_kernel,
        (x0, x2, xn, d0, d2, dn, u0, u1, u2, u3_low, u3_high, mod, stat, qk, soft, weights, back_w, back_late),
        (terms,) * 4 + (((F, 128), F32),),
        (vmem((4, 2 * F, W), BF), vmem((2 * F, W), BF), vmem((2 * F, W), BF), vmem((4, 2 * F, W), F32),
         vmem((4, F, W), BF)), 20, "tangent", 1 << 34)
    beside = swap_core(u1)
    score, = local_call(
        score_kernel, (u0, beside, got_first, got_rest, x0, mod, stat), (((F * 16, 128), BF),), (vmem((F * 16, 128), F32),), 6, "score")
    v_far, v_near = swap_core(v3), swap_core(v1)
    v_sum, = local_call(add_kernel, (got_rest, v2, v_far), (terms,), (), 4, "add")
    v_chip = swap_chip(v_sum)

    ready, = local_call(
        finish_kernel, (score, v0, v_near, v_chip), (((F * 24, 128), BF),), (vmem((F, 24, 128), F32),), 6, "finish")
    back = lax.all_to_all(ready, "seq", split_axis=0, concat_axis=0, tiled=True)
    score_field, table = local_call(
        tail_kernel, (back, ids_late), (((2 * F, W), BF), ((16, CONCEPTS), F32)),
        (vmem((F * 24, 128), F32), vmem((2 * F * 8, 128), F32)), 8, "tail")
    return (score_field.reshape(1, 2 * F, W), table.T)


def solution(mesh):
    in_specs = (
        P("seq", None, "tp"),
        P("seq", None, "tp"),
        P("seq"),
        P(),
        P(None, "tp"),
        P(None, "tp"),
        P(None, "tp"),
    )
    out_specs = (P("seq", None, "tp"), P(None, ("seq", "tp")))
    return jax.shard_map(body, mesh=mesh, in_specs=in_specs, out_specs=out_specs, check_vma=False)
```

```python
import math

import jax
import jax.numpy as jnp
from jax import lax
from jax.experimental import pallas as pl
from jax.experimental.pallas import tpu as pltpu
from jax.sharding import PartitionSpec as P

D = 4096
HD = 128
CONCEPTS = 256
STEPS = 1000
EPS = 1e-06
F = 64
W = 1024
STEP = 36

BF = jnp.bfloat16
F32 = jnp.float32
NT = (((1,), (1,)), ((), ()))


def nt(a, b):
    return lax.dot_general(a, b, NT, preferred_element_type=F32)


def turn_kernel(wq_ref, wk_ref, o_ref, token_ref, w_s, t_s, sems, out_sems):
    me = lax.axis_index("tp")
    copies, outs = [], []
    for k in range(4):
        rows = pl.ds(pl.multiple_of((me ^ k) * W, W), W)
        for i, ref in enumerate((wq_ref, wk_ref)):
            copy = pltpu.make_async_copy(ref.at[rows], w_s.at[k, :, pl.ds(512 * i, 512)], sems.at[2 * k + i])
            copy.start()
            copies.append(copy)
    for k in range(4):
        copies[2 * k].wait()
        copies[2 * k + 1].wait()
        for j in range(4):
            t_s[k, :, 256 * j:256 * j + 256] = w_s[k, 256 * j:256 * j + 256, :].T
        out = pltpu.make_async_copy(t_s.at[k], o_ref.at[k], out_sems.at[k])
        out.start()
        outs.append(out)
    for out in outs:
        out.wait()
    token_ref[...] = jnp.zeros_like(token_ref)


def prepare_kernel(wq_ref, wk_ref, turned_ref, table_ref, t1, t2, t3, ids_ref, steps_ref, w_ref, late_ref, mod_ref, t0, sems):
    me = lax.axis_index("tp")
    own = pltpu.make_async_copy(table_ref, t0, sems.at[8])
    own.start()
    copies = []
    for k in range(4):
        rows = pl.ds(pl.multiple_of((me ^ k) * W, W), W)
        for i, ref in enumerate((wq_ref, wk_ref)):
            copy = pltpu.make_async_copy(ref.at[rows], w_ref.at[k, :, pl.ds(512 * i, 512)], sems.at[2 * k + i])
            copy.start()
            copies.append(copy)
    for k in range(3):
        copy = pltpu.make_async_copy(turned_ref.at[1 + k], late_ref.at[k], sems.at[9 + k])
        copy.start()
        copies.append(copy)
    ids = ids_ref[:, 0:128].astype(F32)
    onehot = (ids[:, 0:1] == lax.broadcasted_iota(jnp.int32, (F, CONCEPTS), 1).astype(F32)).astype(BF)
    for k, ref in ((1, t1), (2, t2), (3, t3), (0, t0)):
        if k == 0:
            own.wait()
        mod_ref[k] = 1.0 + jnp.dot(onehot, ref[...], preferred_element_type=F32)
    mod_ref[4, :, 0:128] = ids
    mod_ref[4, :, 128:256] = jnp.zeros((F, 128), F32) + steps_ref[...]
    for copy in copies:
        copy.wait()


def relay_kernel(_, v_ref, o_ref):
    o_ref[...] = v_ref[...]


def join_kernel(_, a_ref, b_ref, o_ref):
    o_ref[0:2] = a_ref[...]
    o_ref[2:4] = b_ref[...]


def slices(own, chip, near):
    return [own.at[0:2], near.at[0:2], chip.at[0:2], near.at[2:4]]


def pack_kernel(x_ref, d_ref, concept_ref, o_ref, x_s, d_s, id_s, in_s, out_s, send_s, sems):
    y_hi = lax.axis_index("tp") >> 1
    copies = [
        pltpu.make_async_copy(src, dst, sems.at[i])
        for i, (src, dst) in enumerate(((x_ref, x_s), (d_ref, d_s), (concept_ref, id_s)))]
    for copy in copies:
        copy.start()
    for half, ref in enumerate((x_s, d_s)):
        copies[half].wait()
        for j in range(8):
            in_s[256 * j + 128 * half:256 * j + 128 * half + 128] = ref[:, 128 * j:128 * j + 128].astype(F32)
        for p in range(2):
            for j in range(8):
                rows = in_s[pl.ds(256 * j + 128 * half + p, F, stride=2), :]
                out_s[pl.ds(j * 4 + 2 * half + p, F, stride=STEP), :] = flip_rows(rows, y_hi)
    copies[2].wait()
    for q in range(4):
        out_s[pl.ds(32 + q, F, stride=STEP), :] = jnp.zeros((F, 128), F32) + id_s[0].astype(F32)
    outs = []
    for i in range(4):
        rows = pl.ds(16 * i, 16)
        send_s[rows] = out_s[16 * STEP * i:16 * STEP * i + 16 * STEP].astype(BF).reshape(16, 9, 4, 128)
        out = pltpu.make_async_copy(send_s.at[rows], o_ref.at[rows], sems.at[3 + i])
        out.start()
        outs.append(out)
    for out in outs:
        out.wait()


def flip_rows(v, y_hi):
    v = v.reshape(8, 8, 128)
    swapped = jnp.concatenate([v[:, 4:8], v[:, 0:4]], axis=1)
    return jnp.where(y_hi == 1, swapped, v).reshape(F, 128)


def unpack_kernel(_, g_ref, x_ref, d_ref, ids_ref, in_s):
    in_s[0:F * STEP] = g_ref[...].reshape(F * STEP, 128).astype(F32)
    for q in range(4):
        ref = (x_ref, d_ref)[q // 2]
        for j in range(8):
            ref[q % 2, :, 128 * j:128 * j + 128] = in_s[pl.ds(j * 4 + q, F, stride=STEP), :].astype(BF)
    ids_ref[:, 0:128] = in_s[pl.ds(32, F, stride=STEP), :].astype(BF)


def tail_kernel(g_ref, ids_ref, score_ref, table_ref, in_s, out_s):
    y_hi = lax.axis_index("tp") >> 1
    in_s[0:F * 24] = g_ref[...].astype(F32)
    for p in range(2):
        for j in range(8):
            rows = in_s[pl.ds(p * 8 + j, F, stride=24), :]
            out_s[pl.ds(128 * j + p, F, stride=2), :] = flip_rows(rows, y_hi)
    for j in range(8):
        score_ref[:, 128 * j:128 * j + 128] = out_s[128 * j:128 * j + 128].astype(BF)
    total = jnp.sum(in_s[0:F * 24].reshape(F, 24, 128)[:, 16:24], axis=0)
    cols = jnp.concatenate([total[:, 0:64], total[:, 64:128]], axis=0)
    ids = ids_ref[:, 0:1]
    onehot = (ids == lax.broadcasted_iota(jnp.int32, (F, CONCEPTS), 1).astype(F32)).astype(F32)
    table_ref[...] = jnp.dot(cols, onehot, precision=lax.Precision.HIGHEST, preferred_element_type=F32)


def forward(h_s, w_ref, out_ref):
    for part in range(4):
        cols = pl.ds(256 * part, 256)
        total = jnp.zeros((2 * F, 256), F32)
        for k in range(4):
            total = total + jnp.dot(h_s[k], w_ref[k, :, cols], preferred_element_type=F32)
        out_ref[:, cols] = total.astype(BF)


def eye128():
    return lax.broadcasted_iota(jnp.int32, (128, 128), 0) == lax.broadcasted_iota(jnp.int32, (128, 128), 1)


def spots():
    return [(pl.ds(64 * p, 64), pl.ds(128 * h, 128), pl.ds(512 + 128 * h, 128)) for p in range(2) for h in range(4)]


def latent_kernel(x0, x2, xn, mod_ref, _, w_ref, late_ref,
                  u2, u3_low, u3_high, qk_ref, soft_ref, stat_ref, g_s, h_s, u3):
    xs = slices(x0, x2, xn)
    sq = jnp.zeros((2 * F, 128), F32)
    for k in range(4):
        for j in range(8):
            x = xs[k][:, :, 128 * j:128 * j + 128].astype(F32).reshape(2 * F, 128)
            sq = sq + x * x
    inv = lax.rsqrt(jnp.sum(sq, axis=-1, keepdims=True) / D + EPS)
    lane = lax.broadcasted_iota(jnp.int32, (2 * F, 128), 1)
    stat_ref[...] = jnp.where(lane == 0, inv, 0.0)
    for k in range(4):
        for j in range(4):
            lanes = pl.ds(256 * j, 256)
            m = mod_ref[k, :, lanes]
            n = xs[k][:, :, lanes].astype(F32).reshape(2 * F, 256) * inv
            h_s[k, :, lanes] = (n * jnp.concatenate([m, m], axis=0)).astype(BF)
    forward(h_s, w_ref, qk_ref)

    temp = mod_ref[4, :, 128:192]
    where = spots()
    qs = [qk_ref[r, ql] for r, ql, _ in where]
    ks = [qk_ref[r, kl] for r, _, kl in where]
    scores = [nt(q, k) * temp for q, k in zip(qs, ks)]
    tops = [jnp.max(v, axis=-1, keepdims=True) for v in scores]
    exps = [jnp.exp(v - t) for v, t in zip(scores, tops)]
    sums = [jnp.sum(e, axis=-1, keepdims=True) for e in exps]
    ws = [e / v for e, v in zip(exps, sums)]
    for i, w in enumerate(ws):
        soft_ref[64 * i:64 * i + 64, :] = w
    gqs = [(-jnp.dot(w.astype(BF), k, preferred_element_type=F32)).astype(BF) for w, k in zip(ws, ks)]
    gks = [(-jnp.dot(w.T.astype(BF), q, preferred_element_type=F32)).astype(BF) for w, q in zip(ws, qs)]
    part = [jnp.zeros((F, HD), F32), jnp.zeros((F, HD), F32)]
    for i, (r, ql, kl) in enumerate(where):
        g_s[r, ql] = gqs[i]
        g_s[r, kl] = gks[i]
        part[i // 4] = part[i // 4] + gqs[i].astype(F32) * qs[i].astype(F32) + gks[i].astype(F32) * ks[i].astype(F32)
    scal = jnp.sum(jnp.concatenate(part, axis=0), axis=-1, keepdims=True)
    srow = jnp.sum(jnp.where(eye128(), scal, 0.0), axis=0, keepdims=True)
    hi = srow.astype(BF).astype(F32)
    sub = lax.broadcasted_iota(jnp.int32, (16, 128), 0)
    stats = jnp.where(sub == 0, hi, jnp.where(sub == 1, srow - hi, 0.0)).astype(BF)
    for ref, k in ((u3, 2), (u2, 1)):
        for j in range(4):
            lanes = pl.ds(256 * j, 256)
            ref[0:128, lanes] = jnp.dot(g_s[...], late_ref[k, :, lanes], preferred_element_type=F32).astype(BF)
        ref[128:144, 0:128] = stats
        ref[128:144, 128:1024] = jnp.zeros((16, 896), BF)
    u3_low[...] = u3[0:64, :]
    u3_high[...] = u3[64:144, :]


def normed_of(x_ref, d_ref, lanes, inv, mean):
    n = x_ref[:, :, lanes].astype(F32).reshape(2 * F, -1) * inv
    d = d_ref[:, :, lanes].astype(F32).reshape(2 * F, -1)
    return n, inv * (d - n * mean)


def tangent_kernel(x0, x2, xn, d0, d2, dn, u0, u1, u2, u3_low, u3_high, mod_ref, stat_ref, qk_ref, soft_ref,
                   w_ref, back_ref, late_ref, o0, o1, o2, o3, ids_ref, h_s, tan_s, g_s, drift_s, term_s):
    xs, ds = slices(x0, x2, xn), slices(d0, d2, dn)
    me = lax.axis_index("tp")
    ids_ref[...] = mod_ref[4, :, 0:128]
    sd = jnp.zeros((2 * F, 128), F32)
    for k in range(4):
        for j in range(8):
            x = xs[k][:, :, 128 * j:128 * j + 128].astype(F32).reshape(2 * F, 128)
            d = ds[k][:, :, 128 * j:128 * j + 128].astype(F32).reshape(2 * F, 128)
            sd = sd + x * d
    inv = jnp.sum(stat_ref[...], axis=-1, keepdims=True)
    mean = inv * (jnp.sum(sd, axis=-1, keepdims=True) / D)

    for k in range(4):
        for j in range(4):
            lanes = pl.ds(256 * j, 256)
            nd = normed_of(xs[k], ds[k], lanes, inv, mean)[1]
            m = mod_ref[k, :, lanes]
            h_s[k, :, lanes] = (nd * jnp.concatenate([m, m], axis=0)).astype(BF)
    forward(h_s, w_ref, tan_s)

    temp = mod_ref[4, :, 128:192]
    where = spots()
    qs = [qk_ref[r, ql] for r, ql, _ in where]
    ks = [qk_ref[r, kl] for r, _, kl in where]
    qts = [tan_s[r, ql] for r, ql, _ in where]
    kts = [tan_s[r, kl] for r, _, kl in where]
    ws = [soft_ref[64 * i:64 * i + 64, :] for i in range(8)]
    tdots = [nt(jnp.concatenate([a, b], axis=1), jnp.concatenate([c, d], axis=1)) for a, b, c, d in zip(qts, qs, ks, kts)]
    means = [jnp.sum(w * t, axis=-1, keepdims=True) for w, t in zip(ws, tdots)]
    curs = [temp * w * (t - m) for w, t, m in zip(ws, tdots, means)]
    cw = [jnp.concatenate([c, w], axis=1).astype(BF) for w, c in zip(ws, curs)]
    cwt = [jnp.concatenate([c, w], axis=0).T.astype(BF) for w, c in zip(ws, curs)]
    aqs = [jnp.dot(m, jnp.concatenate([k, kt], axis=0), preferred_element_type=F32) for m, k, kt in zip(cw, ks, kts)]
    aks = [jnp.dot(m, jnp.concatenate([q, qt], axis=0), preferred_element_type=F32) for m, q, qt in zip(cwt, qs, qts)]
    for i, (r, ql, kl) in enumerate(where):
        g_s[r, ql] = (-aqs[i]).astype(BF)
        g_s[r, kl] = (-aks[i]).astype(BF)

    for k in range(4):
        for j in range(4):
            lanes = pl.ds(256 * j, 256)
            block = back_ref[:, lanes] if k == 0 else late_ref[k - 1, :, lanes]
            drift_s[k, :, lanes] = jnp.dot(g_s[...], block, preferred_element_type=F32)

    rr = lax.broadcasted_iota(jnp.int32, (128, 256), 0)
    cc = lax.broadcasted_iota(jnp.int32, (128, 256), 1)
    pick = (((rr >> 3) & 3) == (cc >> 6)) & ((rr >> 5) == ((cc >> 4) & 3)) & ((rr & 7) == (cc & 7))
    pick = pick.astype(BF)
    late = ((lax.broadcasted_iota(jnp.int32, (F, 256), 1) >> 3) & 1) == 1
    for k in range(4):
        for j in range(4):
            lanes = pl.ds(256 * j, 256)
            n, nd = normed_of(xs[k], ds[k], lanes, inv, mean)
            if k == 3:
                units = jnp.concatenate([u3_low[:, lanes], u3_high[0:64, lanes]], axis=0)
            else:
                units = (u0, u1, u2)[k][0:128, lanes]
            terms = n * drift_s[k, :, lanes] + nd * units.astype(F32)
            terms = terms[0:64] + terms[64:128]
            split = jnp.concatenate([jnp.where(late, 0.0, terms), jnp.where(late, terms, 0.0)], axis=0).astype(BF)
            moved = nt(pick, split).astype(BF)
            spot = pl.ds(pl.multiple_of((me ^ k) * 256 + 128 * (j // 2), 128), 128)
            low = 32 * (j % 2)
            for t in range(4):
                term_s[t, low:low + 32, spot] = moved[32 * t:32 * t + 32]
    o0[...] = term_s[me]
    o2[...] = term_s[me ^ 2]
    o3[...] = term_s[me ^ 3]
    o1[...] = term_s[me ^ 1]


def local_call(kernel, args, outs, scratch, limit, name, flops=1 << 12, hbm=0):
    vm = pl.BlockSpec(memory_space=pltpu.VMEM)
    args = [pltpu.with_memory_space_constraint(v, pltpu.HBM) if i < hbm else v for i, v in enumerate(args)]
    return pl.pallas_call(
        kernel,
        out_shape=tuple(jax.ShapeDtypeStruct(s, t) for s, t in outs),
        in_specs=[pl.BlockSpec(memory_space=pltpu.HBM)] * hbm + [vm] * (len(args) - hbm),
        out_specs=tuple(vm for _ in outs),
        scratch_shapes=scratch,
        compiler_params=pltpu.CompilerParams(vmem_limit_bytes=limit * 1024 * 1024),
        cost_estimate=pl.CostEstimate(flops=flops, bytes_accessed=1 << 12, transcendentals=0),
        name=name,
    )(*args)


def add_kernel(_, a_ref, b_ref, o_ref):
    o_ref[...] = (a_ref[...].astype(F32) + b_ref[...].astype(F32)).astype(BF)


def merge_kernel(a_ref, low_ref, high_ref, first_ref, rest_ref):
    first_ref[...] = (a_ref[0:32, :].astype(F32) + low_ref[0:32, :].astype(F32)).astype(BF)
    rest_ref[0:32, :] = (a_ref[32:64, :].astype(F32) + low_ref[32:64, :].astype(F32)).astype(BF)
    rest_ref[32:96, :] = (a_ref[64:128, :].astype(F32) + high_ref[0:64, :].astype(F32)).astype(BF)
    rest_ref[96:112, :] = jnp.concatenate(
        [a_ref[128:144, 0:128], high_ref[64:80, 0:128], a_ref[128:144, 256:1024]], axis=1)


def others_kernel(turned_ref, _, grad_ref, u2, late_ref, back_ref, u0, u1, sem):
    copy = pltpu.make_async_copy(turned_ref.at[0], back_ref, sem)
    copy.start()
    for k, ref in ((1, u1), (0, u0)):
        if k == 0:
            copy.wait()
        for j in range(4):
            lanes = pl.ds(256 * j, 256)
            block = back_ref[:, lanes] if k == 0 else late_ref[0, :, lanes]
            ref[0:128, lanes] = jnp.dot(grad_ref[...], block, preferred_element_type=F32).astype(BF)
        ref[128:144, :] = u2[128:144, :]


def score_kernel(a_ref, b_ref, first_ref, rest_ref, x_ref, mod_ref, stat_ref, score_ref, out_s):
    srow = jnp.zeros((1, 128), F32)
    for ref, row, lane in ((a_ref, 128, 0), (b_ref, 128, 0), (rest_ref, 96, 0), (rest_ref, 96, 128)):
        part = ref[row:row + 16, lane:lane + 128].astype(F32)
        srow = srow + (part[0:1] + part[1:2])
    mean = jnp.sum(jnp.where(eye128(), srow, 0.0), axis=1, keepdims=True) / D
    inv = jnp.sum(stat_ref[...], axis=1, keepdims=True)
    for j in range(4):
        lanes = pl.ds(256 * j, 256)
        far = jnp.concatenate([first_ref[:, lanes], rest_ref[0:96, lanes]], axis=0).astype(F32)
        units = (a_ref[0:128, lanes].astype(F32) + b_ref[0:128, lanes].astype(F32)) + far
        mod = mod_ref[0, :, lanes]
        mod = jnp.concatenate([mod, mod], axis=0)
        x = x_ref[:, :, lanes].astype(F32).reshape(2 * F, 256)
        score = inv * (mod * units - (x * inv) * mean)
        for p in range(2):
            for i in range(2):
                out_s[pl.ds(8 * p + 2 * j + i, F, stride=16), :] = score[64 * p:64 * p + 64, 128 * i:128 * i + 128]
    score_ref[...] = out_s[0:F * 16].astype(BF)


def finish_kernel(score_ref, a_ref, b_ref, c_ref, o_ref, out_s):
    out_s[:, 0:16] = score_ref[...].astype(F32).reshape(F, 16, 128)
    total = (a_ref[...].astype(F32) + b_ref[...].astype(F32)) + c_ref[...].astype(F32)
    for j in range(8):
        out_s[8 * j:8 * j + 8, 16:24] = total[:, 128 * j:128 * j + 128].reshape(8, 8, 128)
    o_ref[...] = out_s[...].reshape(F * 24, 128).astype(BF)


def body(latent, direction, concept, timestep, concept_table, w_query, w_key):
    cross = []
    for s in range(64):
        for t in range(4):
            cross.append((4 * s + t, 4 * (s ^ 4) + (t ^ 2)))
    core = [(t, t ^ 1) for t in range(4)]
    swap_core = lambda v: lax.ppermute(v, "tp", core)
    swap_chip = lambda v: lax.ppermute(v, ("seq", "tp"), cross)
    vmem = pltpu.VMEM

    hbm = pl.BlockSpec(memory_space=pltpu.HBM)
    sent = pl.pallas_call(
        pack_kernel,
        out_shape=jax.ShapeDtypeStruct((F, 9, 4, 128), BF),
        in_specs=[hbm, hbm, pl.BlockSpec(memory_space=pl.ANY)],
        out_specs=hbm,
        scratch_shapes=[
            vmem((2 * F, W), BF), vmem((2 * F, W), BF), pltpu.SMEM((1,), jnp.int32), vmem((4 * F * 8 + 8, 128), F32),
            vmem((F * STEP + 40, 128), F32), vmem((F, 9, 4, 128), BF), pltpu.SemaphoreType.DMA((7,))],
        compiler_params=pltpu.CompilerParams(vmem_limit_bytes=8 * 1024 * 1024),
        name="pack",
    )(*[pltpu.with_memory_space_constraint(v.reshape(2 * F, W), pltpu.HBM) for v in (latent, direction)], concept)
    got = lax.all_to_all(sent, "seq", split_axis=0, concat_axis=0, tiled=True)

    turned, token = pl.pallas_call(
        turn_kernel,
        out_shape=(jax.ShapeDtypeStruct((4, W, W), BF), jax.ShapeDtypeStruct((8, 128), F32)),
        in_specs=[hbm, hbm],
        out_specs=(hbm, pl.BlockSpec(memory_space=pltpu.VMEM)),
        scratch_shapes=[vmem((4, W, W), BF), vmem((4, W, W), BF),
                        pltpu.SemaphoreType.DMA((8,)), pltpu.SemaphoreType.DMA((4,))],
        compiler_params=pltpu.CompilerParams(vmem_limit_bytes=24 * 1024 * 1024),
        cost_estimate=pl.CostEstimate(flops=1 << 33, bytes_accessed=1 << 24, transcendentals=0),
        name="turn",
    )(pltpu.with_memory_space_constraint(w_query, pltpu.HBM), pltpu.with_memory_space_constraint(w_key, pltpu.HBM))
    t_core = swap_core(concept_table)
    t_chip = swap_chip(concept_table)
    t_both = swap_core(t_chip)

    half = ((2, F, W), BF)
    x0, d0, ids = local_call(
        unpack_kernel, (token, got), (half, half, ((F, 2 * W), BF)), (vmem((F * STEP + 40, 128), F32),), 8, "unpack")

    steps = ((0.25 + 1.75 * timestep.astype(F32) / STEPS) / math.sqrt(HD)).reshape(F, 1)
    weights, back_late, mod = local_call(
        prepare_kernel, (w_query, w_key, turned, concept_table, t_core, t_chip, t_both, ids, steps),
        (((4, W, W), BF), ((3, W, W), BF), ((5, F, W), F32)),
        (vmem((CONCEPTS, W), BF), pltpu.SemaphoreType.DMA((12,))), 18, "prepare", 1 << 32, hbm=4)
    full = ((4, F, W), BF)
    join = lambda *v: local_call(join_kernel, v, (full,), (), 4, "join")[0]
    x2 = swap_chip(x0)
    xn = swap_core(join(mod, x0, x2))
    d_out, = local_call(relay_kernel, (x2, d0), (half,), (), 4, "relay")
    d2 = swap_chip(d_out)

    units, terms = ((144, W), BF), ((F, W), BF)
    u2, u3_low, u3_high, qk, soft, stat, grads = local_call(
        latent_kernel, (x0, x2, xn, mod, d_out, weights, back_late),
        (units, terms, ((80, W), BF), ((2 * F, W), BF), ((8 * F, F), F32), ((2 * F, 128), F32), ((2 * F, W), BF)),
        (vmem((4, 2 * F, W), BF), vmem((144, W), BF)), 16, "latents", 1 << 30)
    low, high = swap_core(u3_low), swap_core(u3_high)
    first, rest = local_call(
        merge_kernel, (u2, low, high), (((32, W), BF), ((112, W), BF)), (), 4, "merge")
    back_w, u0, u1 = local_call(
        others_kernel, (turned, first, grads, u2, back_late), (((W, W), BF), units, units), (pltpu.SemaphoreType.DMA,),
        8, "others", 1 << 12, hbm=1)
    dn = swap_core(join(u0, d0, d2))
    got_first = swap_chip(first)
    rest, = local_call(relay_kernel, (got_first, rest), (((112, W), BF),), (), 4, "relay", 1 << 34)
    got_rest = swap_chip(rest)
    v0, v1, v2, v3, ids_late = local_call(
        tangent_kernel,
        (x0, x2, xn, d0, d2, dn, u0, u1, u2, u3_low, u3_high, mod, stat, qk, soft, weights, back_w, back_late),
        (terms,) * 4 + (((F, 128), F32),),
        (vmem((4, 2 * F, W), BF), vmem((2 * F, W), BF), vmem((2 * F, W), BF), vmem((4, 2 * F, W), F32),
         vmem((4, F, W), BF)), 20, "tangent", 1 << 34)
    beside = swap_core(u1)
    score, = local_call(
        score_kernel, (u0, beside, got_first, got_rest, x0, mod, stat), (((F * 16, 128), BF),), (vmem((F * 16 + 16, 128), F32),), 6, "score")
    v_far, v_near = swap_core(v3), swap_core(v1)
    v_sum, = local_call(add_kernel, (got_rest, v2, v_far), (terms,), (), 4, "add")
    v_chip = swap_chip(v_sum)

    ready, = local_call(
        finish_kernel, (score, v0, v_near, v_chip), (((F * 24, 128), BF),), (vmem((F, 24, 128), F32),), 6, "finish")
    back = lax.all_to_all(ready, "seq", split_axis=0, concat_axis=0, tiled=True)
    score_field, table = local_call(
        tail_kernel, (back, ids_late), (((2 * F, W), BF), ((16, CONCEPTS), F32)),
        (vmem((F * 24 + 24, 128), F32), vmem((2 * F * 8 + 8, 128), F32)), 8, "tail")
    return (score_field.reshape(1, 2 * F, W), table.T)


def solution(mesh):
    in_specs = (
        P("seq", None, "tp"),
        P("seq", None, "tp"),
        P("seq"),
        P(),
        P(None, "tp"),
        P(None, "tp"),
        P(None, "tp"),
    )
    out_specs = (P("seq", None, "tp"), P(None, ("seq", "tp")))
    return jax.shard_map(body, mesh=mesh, in_specs=in_specs, out_specs=out_specs, check_vma=False)
```
